512 devices in a mesh: seq: 512 (over x, y, z, core).
Axes of the slice: x: 4, y: 8, z: 8, core: 2. Of those that a mesh axis runs over, the one named last changes fastest.
Arguments:
- right_side: bfloat16 [262144, 384], P('seq'), may hold values from -6 to 6
- leaf_inverse: bfloat16 [512, 512, 512], P('seq'), may hold values from -1 to 2
- project_rows: bfloat16 [9, 262144, 128], P(None, 'seq'), may hold values from -3 to 3, as said below
- spread_rows: bfloat16 [9, 262144, 128], P(None, 'seq'), may hold values from -0.119628906 to 0.119628906
- capacity: bfloat16 [9, 65536, 256], P(None, 'seq'), may hold values from -1 to 2, as said below
Outputs:
- solution: float32 [262144, 384], P('seq')
The draws below stay inside these ranges and needn't reach their ends.
Inputs may be any that keep to these rules, and one draw needn't show every extreme that they name: Rows of project_rows of level l have a scale falling as (2 ** l * 512) ** -0.5. `capacity`: at level l the 128 x 2 * 128 blocks of all devices in one half of a node of 2 ** (l + 1) devices are equal.
All inputs are finite; a program needn't handle non-finite values.
Results may differ from the reference program's by a relative error of at most 0.0095.
Values may be sent and summed in bfloat16 or wider, within the bound.
No kernel may reach another device: no remote copies, remote signals or barrier semaphores. Data moves between devices by JAX's collectives and lax.ppermute only.
A program may use at most 64 MiB of HBM per device.

```python
import math
import jax
import jax.numpy as jnp
from jax import lax

SEG = 512
R = 128
RHS = 384
SAMPLES = 262144
LEVELS = 9
N_SEQ = 512


def draw_leaf_inverse(key, part):
    gaussian = jnp.clip(jax.random.normal(key, (N_SEQ, SEG, SEG), jnp.float32), -4.0, 4.0)
    return (0.6 * jnp.eye(SEG, dtype=jnp.float32) + gaussian / math.sqrt(SEG)).astype(jnp.bfloat16)


def draw_project_rows(key, part):
    layers = []
    for tree_level in range(LEVELS):
        subkey = jax.random.fold_in(key, 101 + tree_level)
        gaussian = jnp.clip(jax.random.normal(subkey, (N_SEQ * SEG, R), jnp.float32), -4.0, 4.0)
        layers.append(gaussian / math.sqrt(SEG * 2 ** tree_level))
    return jnp.stack(layers).astype(jnp.bfloat16)


def draw_capacity(key, part):
    layers = []
    for tree_level in range(LEVELS):
        half_span = 2 ** tree_level
        half_count = N_SEQ // half_span
        subkey = jax.random.fold_in(key, 211 + tree_level)
        gaussian = jnp.clip(jax.random.normal(subkey, (half_count, R, 2 * R), jnp.float32), -4.0, 4.0)
        sides = jnp.arange(half_count) % 2
        column_ids = jnp.arange(2 * R)[None, None, :]
        row_ids = jnp.arange(R)[None, :, None]
        diagonal = (column_ids == row_ids + sides[:, None, None] * R).astype(jnp.float32)
        blocks = 0.6 * diagonal + 0.8 * gaussian / math.sqrt(2 * R)
        blocks = jnp.repeat(blocks, half_span, axis=0)
        layers.append(blocks.reshape(N_SEQ * R, 2 * R))
    return jnp.stack(layers).astype(jnp.bfloat16)


def levels(stream_key, extent, cuts, low, top_value):
    level = 1.0
    for position, blocks in cuts:
        steps = jax.random.uniform(jax.random.fold_in(jax.random.fold_in(stream_key, 6), position), (blocks,), jnp.float32, low / len(cuts), top_value / len(cuts))
        level = level * jnp.repeat(jnp.exp(steps), extent[position] // blocks).reshape((-1,) + (1,) * (len(extent) - 1 - position))
    return level


def normal_values(rng, shape, spread, most, cuts=(), kind=jnp.bfloat16):
    array = jax.random.normal(rng, shape, jnp.float32) * spread
    if len(cuts) > 0:
        array = levels(rng, shape, cuts, -0.22, 0.18) * array
    return jnp.clip(array, min=-most, max=most).astype(kind)


def setup_inputs(seed: int = 0) -> dict:
    keys = jax.random.split(jax.random.key(seed), 6)
    return {
        "right_side": normal_values(keys[0], (SAMPLES, RHS), 1.0, 6.0, ((0, 512),)),
        "leaf_inverse": draw_leaf_inverse(jax.random.fold_in(keys[5], 71), 0),
        "project_rows": draw_project_rows(jax.random.fold_in(keys[5], 71), 0),
        "spread_rows": normal_values(keys[3], (LEVELS, SAMPLES, R), 0.03, 0.119628906, ((1, 512),)),
        "capacity": draw_capacity(jax.random.fold_in(keys[5], 71), 0),
    }


def reference(right_side, leaf_inverse, project_rows, spread_rows, capacity):
    loaded = right_side.reshape(N_SEQ, SEG, RHS).astype(jnp.float32)
    solution = jnp.einsum("dij,djk->dik", leaf_inverse.astype(jnp.float32), loaded)
    for tree_level in range(LEVELS):
        half_span = 2 ** tree_level
        node_count = N_SEQ // (2 * half_span)
        rounded = lax.optimization_barrier(solution.astype(jnp.bfloat16)).astype(jnp.float32)
        basis_rows = project_rows[tree_level].reshape(N_SEQ, SEG, R).astype(jnp.float32)
        partial_sum = jnp.einsum("dsr,dsk->drk", basis_rows, rounded)
        node_sums = partial_sum.reshape(node_count, 2, half_span, R, RHS).sum(axis=2)
        stacked = lax.optimization_barrier(node_sums.astype(jnp.bfloat16)).astype(jnp.float32)
        stacked = stacked.reshape(node_count, 2 * R, RHS)
        node_rows = capacity[tree_level].reshape(node_count, 2, half_span, R, 2 * R)[:, :, 0].astype(jnp.float32)
        coefficients = jnp.einsum("nsrj,njk->nsrk", node_rows, stacked)
        coefficients = lax.optimization_barrier(coefficients.astype(jnp.bfloat16)).astype(jnp.float32)
        spread_all = jnp.broadcast_to(coefficients[:, :, None], (node_count, 2, half_span, R, RHS)).reshape(N_SEQ, R, RHS)
        spread_basis = spread_rows[tree_level].reshape(N_SEQ, SEG, R).astype(jnp.float32)
        solution = solution - jnp.einsum("dsr,drk->dsk", spread_basis, spread_all)
    return solution.reshape(N_SEQ * SEG, RHS)
```

```python
import jax
import jax.numpy as jnp
from jax import lax
from jax.experimental import pallas as pl
from jax.experimental.pallas import tpu as pltpu
from jax.sharding import PartitionSpec as P

BF = jnp.bfloat16
F32 = jnp.float32
AXIS = "seq"
MASKS = {3: 12, 6: 96, 8: 384}


def mask_of(level):
    return MASKS.get(level, 1 << level)


def swap(value, mask, core):
    pairs = [(d, d ^ mask) for d in range(lax.axis_size(AXIS)) if d & 1 == core]
    return lax.ppermute(value, AXIS, pairs)


def to_core(value, core):
    pairs = [(d ^ 1, d) for d in range(lax.axis_size(AXIS)) if d & 1 == core]
    return lax.ppermute(value, AXIS, pairs)


def dot(a, b, dims):
    return lax.dot_general(a, b, (dims, ((), ())), preferred_element_type=F32)


NN = ((1,), (0,))
NT = ((1,), (1,))
TN = ((0,), (0,))


def call(body, out_shape, args, in_specs=None, flops=0):
    if in_specs is None:
        in_specs = [None] * len(args)
    specs = [s if s is not None else pl.BlockSpec(memory_space=pltpu.VMEM) for s in in_specs]
    single = not isinstance(out_shape, (list, tuple))
    outs = pl.BlockSpec(memory_space=pltpu.VMEM)
    size = sum(a.size * a.dtype.itemsize for a in args)
    return pl.pallas_call(
        body,
        out_shape=out_shape,
        grid=(1,),
        in_specs=specs,
        out_specs=outs if single else [outs] * len(out_shape),
        compiler_params=pltpu.CompilerParams(vmem_limit_bytes=32 * 2**20),
        cost_estimate=pl.CostEstimate(flops=flops, bytes_accessed=size, transcendentals=0),
    )(*args)


SCALAR = pl.BlockSpec(memory_space=pltpu.SMEM)


def sds(shape, dtype):
    return jax.ShapeDtypeStruct(shape, dtype)


def static_body(project_ref, spread_ref, out_ref):
    levels = project_ref.shape[0]
    at = 0
    for low in range(1, levels - 1):
        spread = spread_ref[low]
        for high in range(low + 1, levels):
            block = dot(spread, project_ref[high], TN)
            out_ref[:, at : at + block.shape[1]] = block.astype(BF)
            at += block.shape[1]


def leaf_body(inverse_ref, right_ref, project_ref, state_ref, sums_ref):
    state = dot(inverse_ref[0], right_ref[...], NN)
    state_ref[...] = state
    sums_ref[...] = dot(project_ref[0], state.astype(BF), TN).astype(BF)


def first_body(state_ref, stacked_ref, capacity_ref, spread_ref, project_ref, next_ref, sums_ref):
    coefficients = dot(capacity_ref[0], stacked_ref[...], NN).astype(BF)
    state = state_ref[...] - dot(spread_ref[0], coefficients, NN)
    next_ref[...] = state
    rounded = state.astype(BF)
    for level in range(1, project_ref.shape[0]):
        block = dot(rounded, project_ref[level], TN)
        rank = block.shape[1]
        sums_ref[:, (level - 1) * rank : level * rank] = block.astype(BF)


def step_body(half_ref, own_ref, other_ref, static_ref, *out_refs):
    rank = static_ref.shape[0] // 2
    width = own_ref.shape[1] - rank
    lower = half_ref[0] == 0
    own, other = own_ref[:, :rank], other_ref[:, :rank]
    stacked = jnp.concatenate([jnp.where(lower, own, other), jnp.where(lower, other, own)], 1)
    capacity = static_ref[:, width : width + 2 * rank]
    coefficients = dot(stacked, capacity, NT).astype(BF)
    out_refs[0][...] = coefficients[:, : out_refs[0].shape[1]]
    if width:
        both = own_ref[:, rank:].astype(F32) + other_ref[:, rank:].astype(F32)
        out_refs[1][...] = (both - dot(coefficients, static_ref[:, :width], NN)).astype(BF)


def last_body(where_ref, state_ref, spread_ref, own_ref, got_ref, out_ref):
    is_first = where_ref[0] == 0
    total = state_ref[...]
    for level in range(1, spread_ref.shape[0]):
        rows = jnp.where(is_first, own_ref[level - 1], got_ref[level - 1])
        total = total - dot(spread_ref[level], rows, NT)
    out_ref[...] = total


def on_device(right_side, leaf_inverse, project_rows, spread_rows, capacity):
    levels, samples, rank = project_rows.shape
    columns = right_side.shape[1]
    device = lax.axis_index(AXIS)

    def bit(level):
        return (device >> level & 1).astype(jnp.int32)

    def level_block(array, level):
        return pl.BlockSpec((1,) + array.shape[1:], lambda i: (level, 0, 0))

    pairs = (levels - 1) * (levels - 2) // 2
    static = call(static_body, sds((rank, pairs * rank), BF), [project_rows, spread_rows])
    static = static + to_core(static, 1)

    state, sums = call(
        leaf_body,
        [sds((samples, columns), F32), sds((rank, columns), BF)],
        [leaf_inverse, right_side, project_rows],
        [None, None, level_block(project_rows, 0)],
    )
    size = lax.axis_size(AXIS)
    stacked = lax.all_gather(
        sums, AXIS, axis_index_groups=[[d, d + 1] for d in range(0, size, 2)], tiled=True
    )
    state, sums = call(
        first_body,
        [sds((samples, columns), F32), sds((columns, (levels - 1) * rank), BF)],
        [state, stacked, capacity, spread_rows, project_rows],
        [None, None, level_block(capacity, 0), level_block(spread_rows, 0), None],
    )
    sums = sums + to_core(sums, 0)
    half = columns // 2
    side = bit(1)
    own = lax.dynamic_slice_in_dim(sums, side * half, half, 0)
    send = lax.dynamic_slice_in_dim(sums, (1 - side) * half, half, 0)

    gathered = []
    for level in range(1, levels):
        other = swap(send, mask_of(level), 0)

        width = (levels - 1 - level) * rank
        block = jnp.concatenate([static[:, :width], capacity[level]], 1)
        if level < levels - 1:
            message = jnp.concatenate([block, static[:, width:]], 1)
        else:
            message = block
        got = swap(message, mask_of(level), 1)
        cut = width + 2 * rank
        both = jnp.concatenate([block, got[:, :cut]], 0)
        static = static[:, width:] + got[:, cut:]
        both = to_core(both, 0)

        outs = [sds((half, 2 * rank if level == 1 else rank), BF)]
        if width:
            outs.append(sds((half, width), BF))
        results = call(
            step_body, outs, [bit(level)[None], own, other, both], [SCALAR, None, None, None]
        )
        gathered.append(results[0])
        if width:
            own = send = results[1]

    mine = jnp.stack([gathered[0][:, :rank]] + gathered[1:])
    theirs = swap(jnp.stack([gathered[0][:, rank:]] + gathered[1:]), 2, 0)
    both = jnp.where(
        side == 0, jnp.concatenate([mine, theirs], 1), jnp.concatenate([theirs, mine], 1)
    )
    got = to_core(both, 1)
    return call(
        last_body,
        sds((samples, columns), F32),
        [bit(0)[None], state, spread_rows, both, got],
        [SCALAR, None, None, None, None],
    )


def solution(mesh):
    return jax.shard_map(
        on_device,
        mesh=mesh,
        in_specs=(
            P(AXIS, None),
            P(AXIS, None, None),
            P(None, AXIS, None),
            P(None, AXIS, None),
            P(None, AXIS, None),
        ),
        out_specs=P(AXIS, None),
        check_vma=False,
    )
```

```python
import jax
import jax.numpy as jnp
from jax import lax
from jax.experimental import pallas as pl
from jax.experimental.pallas import tpu as pltpu
from jax.sharding import PartitionSpec as P

BF = jnp.bfloat16
F32 = jnp.float32
AXIS = "seq"
MASKS = {3: 12, 6: 96, 8: 384}


def mask_of(level):
    return MASKS.get(level, 1 << level)


def swap(value, mask, core):
    pairs = [(d, d ^ mask) for d in range(lax.axis_size(AXIS)) if d & 1 == core]
    return lax.ppermute(value, AXIS, pairs)


def to_core(value, core, mask=1):
    pairs = [(d ^ mask, d) for d in range(lax.axis_size(AXIS)) if d & 1 == core]
    return lax.ppermute(value, AXIS, pairs)


def dot(a, b, dims):
    return lax.dot_general(a, b, (dims, ((), ())), preferred_element_type=F32)


NN = ((1,), (0,))
NT = ((1,), (1,))
TN = ((0,), (0,))


def call(body, out_shape, args, in_specs=None, flops=0):
    if in_specs is None:
        in_specs = [None] * len(args)
    specs = [s if s is not None else pl.BlockSpec(memory_space=pltpu.VMEM) for s in in_specs]
    single = not isinstance(out_shape, (list, tuple))
    outs = pl.BlockSpec(memory_space=pltpu.VMEM)
    size = sum(a.size * a.dtype.itemsize for a in args)
    return pl.pallas_call(
        body,
        out_shape=out_shape,
        grid=(1,),
        in_specs=specs,
        out_specs=outs if single else [outs] * len(out_shape),
        compiler_params=pltpu.CompilerParams(vmem_limit_bytes=32 * 2**20),
        cost_estimate=pl.CostEstimate(flops=flops, bytes_accessed=size, transcendentals=0),
    )(*args)


SCALAR = pl.BlockSpec(memory_space=pltpu.SMEM)


def sds(shape, dtype):
    return jax.ShapeDtypeStruct(shape, dtype)


def front_body(inverse_ref, right_ref, project_ref, spread_ref, static_ref, state_ref, sums_ref):
    levels = project_ref.shape[0]
    at = 0
    for low in range(1, levels - 1):
        spread = spread_ref[low]
        for high in range(low + 1, levels):
            block = dot(spread, project_ref[high], TN)
            static_ref[:, at : at + block.shape[1]] = block.astype(BF)
            at += block.shape[1]
    state = dot(inverse_ref[0], right_ref[...], NN)
    state_ref[...] = state
    sums_ref[...] = dot(project_ref[0], state.astype(BF), TN).astype(BF)


def first_body(state_ref, stacked_ref, capacity_ref, spread_ref, project_ref, next_ref, sums_ref):
    coefficients = dot(capacity_ref[0], stacked_ref[...], NN).astype(BF)
    state = state_ref[...] - dot(spread_ref[0], coefficients, NN)
    next_ref[...] = state
    rounded = state.astype(BF)
    for level in range(1, project_ref.shape[0]):
        block = dot(rounded, project_ref[level], TN)
        rank = block.shape[1]
        sums_ref[:, (level - 1) * rank : level * rank] = block.astype(BF)


def rows_of(part, count):
    return pl.ds(pl.multiple_of(part * count, count), count)


def merge_body(side_ref, own_ref, other_ref, keep_ref, send_ref):
    side = side_ref[0]
    count = keep_ref.shape[0]
    for part, out_ref in ((side, keep_ref), (1 - side, send_ref)):
        rows = rows_of(part, count)
        total = own_ref[rows, :].astype(F32) + other_ref[rows, :].astype(F32)
        out_ref[...] = total.astype(BF)


def cut_body(side_ref, own_ref, other_ref, capacity_ref, first_ref, keep_ref, send_ref):
    side = side_ref[0]
    width = first_ref.shape[1] - capacity_ref.shape[2]
    first = own_ref[:, :width].astype(F32) + other_ref[:, :width].astype(F32)
    first_ref[:, :width] = first.astype(BF)
    first_ref[:, width:] = capacity_ref[0]
    count = keep_ref.shape[0]
    for part, out_ref in ((side, keep_ref), (1 - side, send_ref)):
        rows = rows_of(part, count)
        total = own_ref[rows, width:].astype(F32) + other_ref[rows, width:].astype(F32)
        out_ref[...] = total.astype(BF)


def static_body(side_ref, own_ref, other_ref, capacity_ref, *out_refs, cut, width):
    message_ref = out_refs[0]
    count = own_ref.shape[0]
    inner = capacity_ref.shape[2]
    if width:
        total = own_ref[:, cut : cut + width].astype(F32) + other_ref[:, cut : cut + width].astype(F32)
        message_ref[:, :width] = total.astype(BF)
    message_ref[:, width : width + inner] = capacity_ref[0, rows_of(side_ref[0], count), :]
    if own_ref.shape[1] > cut + width:
        rest = own_ref[:, cut + width :].astype(F32) + other_ref[:, cut + width :].astype(F32)
        message_ref[:, width + inner :] = rest.astype(BF)
    if cut:
        out_refs[1][:count, :] = own_ref[:, :cut]
        out_refs[1][count:, :] = other_ref[:, :cut]


def step_body(place_ref, own_ref, other_ref, near_ref, far_ref, *out_refs):
    rank = near_ref.shape[0]
    width = own_ref.shape[1] - rank
    lower = place_ref[0] == 0
    own, other = own_ref[:, :rank], other_ref[:, :rank]
    stacked = jnp.concatenate([jnp.where(lower, own, other), jnp.where(lower, other, own)], 1)
    near = dot(stacked, near_ref[:, width:], NT).astype(BF)
    far = dot(stacked, far_ref[:, width:], NT).astype(BF)
    if out_refs[0].shape[1] > rank:
        out_refs[0][:, :rank] = near
        out_refs[0][:, rank:] = far
    else:
        first = place_ref[1] == 0
        part = rank // 2
        near_own, far_own = near[:, :part], far[:, :part]
        out_refs[0][...] = jnp.concatenate(
            [jnp.where(first, near_own, far_own), jnp.where(first, far_own, near_own)], 1
        )
    if width:
        total = own_ref[:, rank:].astype(F32) + other_ref[:, rank:].astype(F32)
        total = total - dot(near, near_ref[:, :width], NN)
        total = total - dot(far, far_ref[:, :width], NN)
        out_refs[1][...] = total.astype(BF)


def spread_body(place_ref, state_ref, spread_ref, near0_ref, far0_ref, near1_ref, far1_ref, out_ref, *, base):
    zero_core = place_ref[0] == 0
    first = place_ref[1] == 0
    total = state_ref[...]
    for index in range(near0_ref.shape[0]):
        near = jnp.where(zero_core, near0_ref[index], near1_ref[index])
        far = jnp.where(zero_core, far0_ref[index], far1_ref[index])
        spread = spread_ref[base + index]
        rows = jnp.concatenate([jnp.where(first, near, far), jnp.where(first, far, near)], 0)
        total = total - dot(spread, rows, NT)
    out_ref[...] = total


def on_device(right_side, leaf_inverse, project_rows, spread_rows, capacity):
    levels, samples, rank = project_rows.shape
    columns = right_side.shape[1]
    inner = capacity.shape[2]
    size = lax.axis_size(AXIS)
    device = lax.axis_index(AXIS)

    def bit(level):
        return (device >> level & 1).astype(jnp.int32)

    def level_block(array, level):
        return pl.BlockSpec((1,) + array.shape[1:], lambda i: (level, 0, 0))

    core, side = bit(0), bit(1)
    pairs = (levels - 1) * (levels - 2) // 2
    static, state, sums = call(
        front_body,
        [sds((rank, pairs * rank), BF), sds((samples, columns), F32), sds((rank, columns), BF)],
        [leaf_inverse, right_side, project_rows, spread_rows],
    )
    static_other = to_core(static, 1)
    stacked = lax.all_gather(
        sums, AXIS, axis_index_groups=[[d, d + 1] for d in range(0, size, 2)], tiled=True
    )
    width = (levels - 2) * rank
    part = rank // 2
    first, keep, send = call(
        cut_body,
        [
            sds((rank, width + inner), BF),
            sds((part, pairs * rank - width), BF),
            sds((part, pairs * rank - width), BF),
        ],
        [side[None], static, static_other, capacity],
        [SCALAR, None, None, level_block(capacity, 1)],
    )
    static_got = swap(send, 2, 1)
    near, far = to_core(first, 0), to_core(first, 0, 3)

    state, sums = call(
        first_body,
        [sds((samples, columns), F32), sds((columns, (levels - 1) * rank), BF)],
        [state, stacked, capacity, spread_rows, project_rows],
        [None, None, level_block(capacity, 0), level_block(spread_rows, 0), None],
    )
    half = columns // 2
    own, send = call(
        merge_body,
        [sds((half, (levels - 1) * rank), BF)] * 2,
        [side[None], sums, to_core(sums, 0)],
        [SCALAR, None, None],
    )

    def spread_out(state, mine, base):
        near0 = jnp.stack([c[:, :rank] for c in mine])
        theirs = jnp.stack([c[:, -rank:] for c in mine])
        far0 = swap(theirs, 2, 0)
        near1 = to_core(near0, 1)
        far1 = to_core(theirs, 1, 3)
        return call(
            lambda *refs: spread_body(*refs, base=base),
            sds((samples, columns), F32),
            [jnp.stack([core, side]), state, spread_rows, near0, far0, near1, far1],
            [SCALAR] + [None] * 6,
        )

    gathered = []
    early = levels - 3
    message, cut = keep, 0
    for level in range(1, levels):
        other = swap(send, mask_of(level), 0)
        if level < levels - 1:
            width = (levels - 2 - level) * rank
            total = message.shape[1] - cut + inner
            outs = [sds((part, total), BF)] + ([sds((rank, cut), BF)] if cut else [])
            results = call(
                lambda *refs, c=cut, w=width: static_body(*refs, cut=c, width=w),
                outs,
                [side[None], message, static_got, capacity],
                [SCALAR, None, None, level_block(capacity, level + 1)],
            )
            message = results[0]
            static_got = swap(message, mask_of(level + 1), 1)
            both = results[1] if cut else None
            cut = width + inner
        else:
            both = jnp.concatenate([message, static_got], 0)
        if level > 1:
            near, far = to_core(both, 0), to_core(both, 0, 3)

        width = (levels - 1 - level) * rank
        outs = [sds((half, 2 * rank if level == 1 else rank), BF)]
        if width:
            outs.append(sds((half, width), BF))
        results = call(
            step_body,
            outs,
            [jnp.stack([bit(level), side]), own, other, near, far],
            [SCALAR, None, None, None, None],
        )
        gathered.append(results[0])
        if width:
            own = send = results[1]
        if level == early:
            state = spread_out(state, gathered, 1)
    return spread_out(state, gathered[early:], early + 1)


def solution(mesh):
    return jax.shard_map(
        on_device,
        mesh=mesh,
        in_specs=(
            P(AXIS, None),
            P(AXIS, None, None),
            P(None, AXIS, None),
            P(None, AXIS, None),
            P(None, AXIS, None),
        ),
        out_specs=P(AXIS, None),
        check_vma=False,
    )
```

```python
import jax
import jax.numpy as jnp
from jax import lax
from jax.experimental import pallas as pl
from jax.experimental.pallas import tpu as pltpu
from jax.sharding import PartitionSpec as P

BF = jnp.bfloat16
F32 = jnp.float32
AXIS = "seq"
MASKS = {3: 12, 6: 96, 8: 384}


def mask_of(level):
    return MASKS.get(level, 1 << level)


def swap(value, mask, core):
    pairs = [(d, d ^ mask) for d in range(lax.axis_size(AXIS)) if d & 1 == core]
    return lax.ppermute(value, AXIS, pairs)


def to_core(value, core, mask=1):
    pairs = [(d ^ mask, d) for d in range(lax.axis_size(AXIS)) if d & 1 == core]
    return lax.ppermute(value, AXIS, pairs)


def dot(a, b, dims):
    return lax.dot_general(a, b, (dims, ((), ())), preferred_element_type=F32)


NN = ((1,), (0,))
NT = ((1,), (1,))
TN = ((0,), (0,))


SMEM = pl.BlockSpec(memory_space=pltpu.SMEM)
VMEM = pl.BlockSpec(memory_space=pltpu.VMEM)
HBM = pl.BlockSpec(memory_space=pltpu.HBM)
ANY = pl.BlockSpec(memory_space=pl.ANY)


def call(body, outs, args, specs, scratch=(), grid=(1,), out_specs=None, limit=40):
    return pl.pallas_call(
        body,
        out_shape=outs,
        grid=grid,
        in_specs=specs,
        out_specs=out_specs or [VMEM] * len(outs),
        scratch_shapes=list(scratch),
        compiler_params=pltpu.CompilerParams(vmem_limit_bytes=limit * 2**20),
        cost_estimate=pl.CostEstimate(
            flops=0, bytes_accessed=sum(a.size * a.dtype.itemsize for a in args), transcendentals=0
        ),
    )(*args)


def sds(shape, dtype):
    return jax.ShapeDtypeStruct(shape, dtype)


def like(array):
    return pltpu.VMEM(array.shape, array.dtype)


def rows_of(part, count):
    return pl.ds(pl.multiple_of(part * count, count), count)


def front_body(
    inverse_hbm, right_hbm, project_hbm, spread_hbm, static_ref, state_ref, sums_ref,
    inverse, right, project, spread, project_sems, spread_sems, inverse_sem, right_sem,
):
    levels = project.shape[0]
    copies = {}
    for level in range(1, levels):
        if level < levels - 1:
            copies["s", level] = pltpu.make_async_copy(spread_hbm.at[level], spread.at[level], spread_sems.at[level])
            copies["s", level].start()
        if level > 1:
            copies["p", level] = pltpu.make_async_copy(project_hbm.at[level], project.at[level], project_sems.at[level])
            copies["p", level].start()
    late = [
        pltpu.make_async_copy(inverse_hbm.at[0], inverse, inverse_sem),
        pltpu.make_async_copy(right_hbm, right, right_sem),
        pltpu.make_async_copy(project_hbm.at[0], project.at[0], project_sems.at[0]),
    ]
    for copy in late:
        copy.start()
    for copy in copies.values():
        copy.wait()
    at = 0
    for low in range(1, levels - 1):
        block = [dot(spread[low], project[high], TN) for high in range(low + 1, levels)]
        for part in block:
            static_ref[:, at : at + part.shape[1]] = part.astype(BF)
            at += part.shape[1]
    for copy in late:
        copy.wait()
    state = dot(inverse[...], right[...], NN)
    state_ref[...] = state
    sums_ref[...] = dot(project[0], state.astype(BF), TN).astype(BF)


def first_body(state_ref, stacked_ref, capacity_ref, spread_ref, project_ref, first_ref, sums_ref):
    coefficients = dot(capacity_ref[0], stacked_ref[...], NN).astype(BF)
    first_ref[...] = coefficients
    rounded = (state_ref[...] - dot(spread_ref[0], coefficients, NN)).astype(BF)
    for level in range(1, project_ref.shape[0]):
        block = dot(rounded, project_ref[level], TN)
        rank = block.shape[1]
        sums_ref[:, (level - 1) * rank : level * rank] = block.astype(BF)


def fetch(pairs, sems):
    copies = [pltpu.make_async_copy(a, b, sems.at[i]) for i, (a, b) in enumerate(pairs)]
    for copy in copies:
        copy.start()
    for copy in copies:
        copy.wait()


def merge_body(bits_ref, own_any, other_any, keep_ref, send_ref, own, other, sems):
    @pl.when(bits_ref[0] == 0)
    def _():
        fetch([(own_any, own), (other_any, other)], sems)
        side = bits_ref[1]
        count = keep_ref.shape[0]
        for part, out_ref in ((side, keep_ref), (1 - side, send_ref)):
            rows = rows_of(part, count)
            out_ref[...] = (own[rows, :].astype(F32) + other[rows, :].astype(F32)).astype(BF)


def cut_body(bits_ref, own_any, other_any, capacity_ref, first_ref, keep_ref, send_ref, own, other, sems):
    @pl.when(bits_ref[0] == 1)
    def _():
        fetch([(own_any, own), (other_any, other)], sems)
        side = bits_ref[1]
        width = first_ref.shape[1] - capacity_ref.shape[2]
        first_ref[:, :width] = (own[:, :width].astype(F32) + other[:, :width].astype(F32)).astype(BF)
        first_ref[:, width:] = capacity_ref[0]
        count = keep_ref.shape[0]
        for part, out_ref in ((side, keep_ref), (1 - side, send_ref)):
            rows = rows_of(part, count)
            total = own[rows, width:].astype(F32) + other[rows, width:].astype(F32)
            out_ref[...] = total.astype(BF)


def static_body(bits_ref, own_any, other_any, capacity_ref, *refs, cut, width, outs):
    out_refs, (own, other, sems) = refs[:outs], refs[outs:]

    @pl.when(bits_ref[0] == 1)
    def _():
        fetch([(own_any, own), (other_any, other)], sems)
        count = own.shape[0]
        inner = capacity_ref.shape[2]
        if cut:
            out_refs[0][:count, :] = own[:, :cut]
            out_refs[0][count:, :] = other[:, :cut]
        if outs == 1 and cut:
            return
        message_ref = out_refs[-1]
        if width:
            total = own[:, cut : cut + width].astype(F32) + other[:, cut : cut + width].astype(F32)
            message_ref[:, :width] = total.astype(BF)
        message_ref[:, width : width + inner] = capacity_ref[0, rows_of(bits_ref[1], count), :]
        if own.shape[1] > cut + width:
            rest = own[:, cut + width :].astype(F32) + other[:, cut + width :].astype(F32)
            message_ref[:, width + inner :] = rest.astype(BF)


def step_body(bits_ref, own_ref, other_ref, near_ref, far_ref, *out_refs, level):
    rank = near_ref.shape[0]
    width = own_ref.shape[1] - rank

    @pl.when(bits_ref[0] == 0)
    def _():
        lower = bits_ref[level] == 0
        own, other = own_ref[:, :rank], other_ref[:, :rank]
        stacked = jnp.concatenate([jnp.where(lower, own, other), jnp.where(lower, other, own)], 1)
        capacity = jnp.concatenate([near_ref[:, width:], far_ref[:, width:]], 0)
        both = dot(stacked, capacity, NT).astype(BF)
        if level == 1:
            out_refs[0][...] = both
        else:
            first = bits_ref[1] == 0
            part = rank // 2
            near, far = both[:, :part], both[:, rank : rank + part]
            out_refs[0][...] = jnp.concatenate([jnp.where(first, near, far), jnp.where(first, far, near)], 1)
        if width:
            total = own_ref[:, rank:].astype(F32) + other_ref[:, rank:].astype(F32)
            static = jnp.concatenate([near_ref[:, :width], far_ref[:, :width]], 0)
            out_refs[1][...] = (total - dot(both, static, NN)).astype(BF)


def spread_body(bits_ref, state_ref, *refs, count, zero):
    spreads, (near0_ref, far0_ref, near1_ref, far1_ref), rest = refs[:count], refs[count : count + 4], refs[count + 4 :]
    out_ref = rest[-1]
    zero_core = bits_ref[0] == 0
    first = bits_ref[1] == 0
    total = state_ref[...]
    if zero:
        total = total - dot(rest[0][0], rest[1][...], NN)
    for at in range(0, count, 2):
        left, right = [], []
        for index in range(at, min(at + 2, count)):
            near = jnp.where(zero_core, near0_ref[index], near1_ref[index])
            far = jnp.where(zero_core, far0_ref[index], far1_ref[index])
            left.append(spreads[index][0])
            right.append(jnp.concatenate([jnp.where(first, near, far), jnp.where(first, far, near)], 0))
        total = total - dot(jnp.concatenate(left, 1), jnp.concatenate(right, 1), NT)
    out_ref[...] = total


def on_device(right_side, leaf_inverse, project_rows, spread_rows, capacity):
    levels, samples, rank = project_rows.shape
    columns = right_side.shape[1]
    inner = capacity.shape[2]
    size = lax.axis_size(AXIS)
    device = lax.axis_index(AXIS)
    bits = (device >> jnp.arange(levels, dtype=jnp.int32) & 1).astype(jnp.int32)
    dma = pltpu.SemaphoreType.DMA

    def level_block(array, level):
        return pl.BlockSpec((1,) + array.shape[1:], lambda i: (level, 0, 0))

    pairs = (levels - 1) * (levels - 2) // 2
    static, state, sums = call(
        front_body,
        [sds((rank, pairs * rank), BF), sds((samples, columns), F32), sds((rank, columns), BF)],
        [leaf_inverse, right_side, project_rows, spread_rows],
        [HBM] * 4,
        [
            pltpu.VMEM(leaf_inverse.shape[1:], BF), like(right_side), like(project_rows), like(spread_rows),
            dma((levels,)), dma((levels,)), dma, dma,
        ],
        limit=60,
    )
    static_other = to_core(static, 1)
    stacked = lax.all_gather(
        sums, AXIS, axis_index_groups=[[d, d + 1] for d in range(0, size, 2)], tiled=True
    )
    width = (levels - 2) * rank
    part = rank // 2
    first, keep, send = call(
        cut_body,
        [
            sds((rank, width + inner), BF),
            sds((part, pairs * rank - width), BF),
            sds((part, pairs * rank - width), BF),
        ],
        [bits, static, static_other, capacity],
        [SMEM, ANY, ANY, level_block(capacity, 1)],
        [like(static), like(static), dma((2,))],
    )
    near, far = to_core(first, 0), to_core(first, 0, 3)

    stacked, send = lax.optimization_barrier((stacked, send))
    static_got = swap(send, 2, 1)
    zero, sums = call(
        first_body,
        [sds((rank, columns), BF), sds((columns, (levels - 1) * rank), BF)],
        [state, stacked, capacity, spread_rows, project_rows],
        [VMEM, VMEM, level_block(capacity, 0), level_block(spread_rows, 0), VMEM],
    )
    half = columns // 2
    own, send = call(
        merge_body,
        [sds((half, (levels - 1) * rank), BF)] * 2,
        [bits, sums, to_core(sums, 0)],
        [SMEM, ANY, ANY],
        [like(sums), like(sums), dma((2,))],
    )

    def spread_out(state, mine, base, zero):
        near0 = jnp.stack([c[:, :rank] for c in mine])
        theirs = jnp.stack([c[:, -rank:] for c in mine])
        far0 = swap(theirs, 2, 0)
        near1 = to_core(near0, 1)
        far1 = to_core(theirs, 1, 3)
        count = len(mine)
        tile = samples // 2

        def spread_block(level):
            return pl.BlockSpec((1, tile, rank), lambda i: (level, i, 0))

        whole = pl.BlockSpec((tile, columns), lambda i: (i, 0))
        args = [bits, state] + [spread_rows] * count + [near0, far0, near1, far1]
        specs = [SMEM, whole] + [spread_block(base + i) for i in range(count)] + [VMEM] * 4
        if zero is not None:
            args += [spread_rows, zero]
            specs += [spread_block(0), VMEM]
        return call(
            lambda *refs: spread_body(*refs, count=count, zero=zero is not None),
            [sds((samples, columns), F32)],
            args,
            specs,
            grid=(2,),
            out_specs=[whole],
        )[0]

    gathered = []
    early = levels - 3
    message, cut = keep, 0
    for level in range(1, levels):
        other = swap(send, mask_of(level), 0)
        if level == 1:
            static_got, near, far, other = lax.optimization_barrier((static_got, near, far, other))
        width = max(levels - 2 - level, 0) * rank
        total = message.shape[1] - cut + inner
        outs = [sds((rank, cut), BF)] if cut else []
        if level < levels - 1:
            outs.append(sds((part, total), BF))
        results = call(
            lambda *refs, c=cut, w=width, n=len(outs): static_body(*refs, cut=c, width=w, outs=n),
            outs,
            [bits, message, static_got, capacity],
            [SMEM, ANY, ANY, level_block(capacity, min(level + 1, levels - 1))],
            [like(message), like(message), dma((2,))],
        )
        if level < levels - 1:
            message = results[-1]
            static_got = swap(message, mask_of(level + 1), 1)
        if level > 1:
            near, far = to_core(results[0], 0), to_core(results[0], 0, 3)
        cut = width + inner

        width = (levels - 1 - level) * rank
        outs = [sds((half, 2 * rank if level == 1 else rank), BF)]
        if width:
            outs.append(sds((half, width), BF))
        results = call(
            lambda *refs, l=level: step_body(*refs, level=l),
            outs,
            [bits, own, other, near, far],
            [SMEM, VMEM, VMEM, VMEM, VMEM],
        )
        gathered.append(results[0])
        if width:
            own = send = results[1]
        if level == early:
            state = spread_out(state, gathered, 1, zero)
    return spread_out(state, gathered[early:], early + 1, None)


def solution(mesh):
    return jax.shard_map(
        on_device,
        mesh=mesh,
        in_specs=(
            P(AXIS, None),
            P(AXIS, None, None),
            P(None, AXIS, None),
            P(None, AXIS, None),
            P(None, AXIS, None),
        ),
        out_specs=P(AXIS, None),
        check_vma=False,
    )
```

```python
import jax
import jax.numpy as jnp
from jax import lax
from jax.experimental import pallas as pl
from jax.experimental.pallas import tpu as pltpu
from jax.sharding import PartitionSpec as P

BF = jnp.bfloat16
F32 = jnp.float32
AXIS = "seq"
MASKS = {3: 12, 6: 96, 8: 384}


def mask_of(level):
    return MASKS.get(level, 1 << level)


def swap(value, mask, core):
    pairs = [(d, d ^ mask) for d in range(lax.axis_size(AXIS)) if d & 1 == core]
    return lax.ppermute(value, AXIS, pairs)


def to_core(value, core, mask=1):
    pairs = [(d ^ mask, d) for d in range(lax.axis_size(AXIS)) if d & 1 == core]
    return lax.ppermute(value, AXIS, pairs)


def dot(a, b, dims):
    return lax.dot_general(a, b, (dims, ((), ())), preferred_element_type=F32)


NN = ((1,), (0,))
NT = ((1,), (1,))
TN = ((0,), (0,))


VMEM = pl.BlockSpec(memory_space=pltpu.VMEM)
ANY = pl.BlockSpec(memory_space=pl.ANY)


def call(body, outs, args, specs, scratch=(), grid=(1,), out_specs=None):
    return pl.pallas_call(
        body,
        out_shape=outs,
        grid=grid,
        in_specs=specs,
        out_specs=out_specs or [VMEM] * len(outs),
        scratch_shapes=list(scratch),
        compiler_params=pltpu.CompilerParams(vmem_limit_bytes=40 * 2**20),
        cost_estimate=pl.CostEstimate(
            flops=0, bytes_accessed=sum(a.size * a.dtype.itemsize for a in args), transcendentals=0
        ),
    )(*args)


def sds(shape, dtype):
    return jax.ShapeDtypeStruct(shape, dtype)


def like(array):
    return pltpu.VMEM(array.shape, array.dtype)


def bit(level):
    return lax.axis_index(AXIS) >> level & 1


def rows_of(part, count):
    return pl.ds(pl.multiple_of(part * count, count), count)


def blocks_body(project_ref, spread_ref, static_ref):
    levels = project_ref.shape[0]
    at = 0
    for low in range(1, levels - 1):
        spread = spread_ref[low]
        for high in range(low + 1, levels):
            block = dot(spread, project_ref[high], TN)
            static_ref[:, at : at + block.shape[1]] = block.astype(BF)
            at += block.shape[1]


def leaf_body(inverse_ref, right_ref, project_ref, state_ref, sums_ref):
    state = dot(inverse_ref[0], right_ref[...], NN)
    state_ref[...] = state
    sums_ref[...] = dot(project_ref[0], state.astype(BF), TN).astype(BF)


def first_body(state_ref, stacked_ref, capacity_ref, spread_ref, project_ref, first_ref, sums_ref):
    coefficients = dot(capacity_ref[0], stacked_ref[...], NN).astype(BF)
    first_ref[...] = coefficients
    rounded = (state_ref[...] - dot(spread_ref[0], coefficients, NN)).astype(BF)
    for level in range(1, project_ref.shape[0]):
        block = dot(rounded, project_ref[level], TN)
        rank = block.shape[1]
        sums_ref[:, (level - 1) * rank : level * rank] = block.astype(BF)


def fetch(pairs, sems):
    copies = [pltpu.make_async_copy(a, b, sems.at[i]) for i, (a, b) in enumerate(pairs)]
    for copy in copies:
        copy.start()
    for copy in copies:
        copy.wait()


def merge_body(own_any, other_any, keep_ref, send_ref, own, other, sems):
    @pl.when(bit(0) == 0)
    def _():
        fetch([(own_any, own), (other_any, other)], sems)
        side = bit(1)
        count = keep_ref.shape[0]
        for part, out_ref in ((side, keep_ref), (1 - side, send_ref)):
            rows = rows_of(part, count)
            out_ref[...] = (own[rows, :].astype(F32) + other[rows, :].astype(F32)).astype(BF)


def cut_body(own_any, other_any, capacity_ref, first_ref, keep_ref, send_ref, own, other, sems):
    @pl.when(bit(0) == 1)
    def _():
        fetch([(own_any, own), (other_any, other)], sems)
        side = bit(1)
        width = first_ref.shape[1] - capacity_ref.shape[2]
        first_ref[:, :width] = (own[:, :width].astype(F32) + other[:, :width].astype(F32)).astype(BF)
        first_ref[:, width:] = capacity_ref[0]
        count = keep_ref.shape[0]
        for part, out_ref in ((side, keep_ref), (1 - side, send_ref)):
            rows = rows_of(part, count)
            total = own[rows, width:].astype(F32) + other[rows, width:].astype(F32)
            out_ref[...] = total.astype(BF)


def static_body(own_any, other_any, capacity_ref, *refs, cut, width, outs):
    out_refs, (own, other, sems) = refs[:outs], refs[outs:]

    @pl.when(bit(0) == 1)
    def _():
        fetch([(own_any, own), (other_any, other)], sems)
        count = own.shape[0]
        inner = capacity_ref.shape[2]
        if cut:
            out_refs[0][:count, :] = own[:, :cut]
            out_refs[0][count:, :] = other[:, :cut]
        if outs == 1 and cut:
            return
        message_ref = out_refs[-1]
        if width:
            total = own[:, cut : cut + width].astype(F32) + other[:, cut : cut + width].astype(F32)
            message_ref[:, :width] = total.astype(BF)
        message_ref[:, width : width + inner] = capacity_ref[0, rows_of(bit(1), count), :]
        if own.shape[1] > cut + width:
            rest = own[:, cut + width :].astype(F32) + other[:, cut + width :].astype(F32)
            message_ref[:, width + inner :] = rest.astype(BF)


def step_body(own_ref, other_ref, near_ref, far_ref, *out_refs, level):
    rank = near_ref.shape[0]
    width = own_ref.shape[1] - rank

    @pl.when(bit(0) == 0)
    def _():
        lower = bit(level) == 0
        own, other = own_ref[:, :rank], other_ref[:, :rank]
        stacked = jnp.concatenate([jnp.where(lower, own, other), jnp.where(lower, other, own)], 1)
        capacity = jnp.concatenate([near_ref[:, width:], far_ref[:, width:]], 0)
        both = dot(stacked, capacity, NT).astype(BF)
        if level == 1:
            out_refs[0][...] = both
        else:
            first = bit(1) == 0
            part = rank // 2
            near, far = both[:, :part], both[:, rank : rank + part]
            out_refs[0][...] = jnp.concatenate([jnp.where(first, near, far), jnp.where(first, far, near)], 1)
        if width:
            total = own_ref[:, rank:].astype(F32) + other_ref[:, rank:].astype(F32)
            static = jnp.concatenate([near_ref[:, :width], far_ref[:, :width]], 0)
            out_refs[1][...] = (total - dot(both, static, NN)).astype(BF)


def spread_body(state_ref, *refs, count, zero):
    spreads, (near0_ref, far0_ref, near1_ref, far1_ref), rest = refs[:count], refs[count : count + 4], refs[count + 4 :]
    out_ref = rest[-1]
    zero_core = bit(0) == 0
    first = bit(1) == 0
    total = state_ref[...]
    if zero:
        total = total - dot(rest[0][0], rest[1][...], NN)
    for at in range(0, count, 2):
        left, right = [], []
        for index in range(at, min(at + 2, count)):
            near = jnp.where(zero_core, near0_ref[index], near1_ref[index])
            far = jnp.where(zero_core, far0_ref[index], far1_ref[index])
            left.append(spreads[index][0])
            right.append(jnp.concatenate([jnp.where(first, near, far), jnp.where(first, far, near)], 0))
        total = total - dot(jnp.concatenate(left, 1), jnp.concatenate(right, 1), NT)
    out_ref[...] = total


def on_device(right_side, leaf_inverse, project_rows, spread_rows, capacity):
    levels, samples, rank = project_rows.shape
    columns = right_side.shape[1]
    inner = capacity.shape[2]
    size = lax.axis_size(AXIS)
    dma = pltpu.SemaphoreType.DMA

    def level_block(array, level):
        return pl.BlockSpec((1,) + array.shape[1:], lambda i: (level, 0, 0))

    pairs = (levels - 1) * (levels - 2) // 2
    (static,) = call(
        blocks_body, [sds((rank, pairs * rank), BF)], [project_rows, spread_rows], [VMEM, VMEM]
    )
    static_other = to_core(static, 1)
    state, sums = call(
        leaf_body,
        [sds((samples, columns), F32), sds((rank, columns), BF)],
        [leaf_inverse, right_side, project_rows],
        [VMEM, VMEM, level_block(project_rows, 0)],
    )
    static_other, sums = lax.optimization_barrier((static_other, sums))
    stacked = lax.all_gather(
        sums, AXIS, axis_index_groups=[[d, d + 1] for d in range(0, size, 2)], tiled=True
    )
    width = (levels - 2) * rank
    part = rank // 2
    first, keep, send = call(
        cut_body,
        [
            sds((rank, width + inner), BF),
            sds((part, pairs * rank - width), BF),
            sds((part, pairs * rank - width), BF),
        ],
        [static, static_other, capacity],
        [ANY, ANY, level_block(capacity, 1)],
        [like(static), like(static), dma((2,))],
    )
    near, far = to_core(first, 0), to_core(first, 0, 3)

    stacked, send = lax.optimization_barrier((stacked, send))
    static_got = swap(send, 2, 1)
    zero, sums = call(
        first_body,
        [sds((rank, columns), BF), sds((columns, (levels - 1) * rank), BF)],
        [state, stacked, capacity, spread_rows, project_rows],
        [VMEM, VMEM, level_block(capacity, 0), level_block(spread_rows, 0), VMEM],
    )
    half = columns // 2
    own, send = call(
        merge_body,
        [sds((half, (levels - 1) * rank), BF)] * 2,
        [sums, to_core(sums, 0)],
        [ANY, ANY],
        [like(sums), like(sums), dma((2,))],
    )

    def spread_out(state, mine, base, zero):
        near0 = jnp.stack([c[:, :rank] for c in mine])
        theirs = jnp.stack([c[:, -rank:] for c in mine])
        far0 = swap(theirs, 2, 0)
        near1 = to_core(near0, 1)
        far1 = to_core(theirs, 1, 3)
        count = len(mine)
        tile = samples // 2

        def spread_block(level):
            return pl.BlockSpec((1, tile, rank), lambda i: (level, i, 0))

        whole = pl.BlockSpec((tile, columns), lambda i: (i, 0))
        args = [state] + [spread_rows] * count + [near0, far0, near1, far1]
        specs = [whole] + [spread_block(base + i) for i in range(count)] + [VMEM] * 4
        if zero is not None:
            args += [spread_rows, zero]
            specs += [spread_block(0), VMEM]
        return call(
            lambda *refs: spread_body(*refs, count=count, zero=zero is not None),
            [sds((samples, columns), F32)],
            args,
            specs,
            grid=(2,),
            out_specs=[whole],
        )[0]

    gathered = []
    early = levels - 3
    message, cut = keep, 0
    for level in range(1, levels):
        other = swap(send, mask_of(level), 0)
        if level == 1:
            static_got, near, far, other = lax.optimization_barrier((static_got, near, far, other))
        width = max(levels - 2 - level, 0) * rank
        total = message.shape[1] - cut + inner
        outs = [sds((rank, cut), BF)] if cut else []
        if level < levels - 1:
            outs.append(sds((part, total), BF))
        results = call(
            lambda *refs, c=cut, w=width, n=len(outs): static_body(*refs, cut=c, width=w, outs=n),
            outs,
            [message, static_got, capacity],
            [ANY, ANY, level_block(capacity, min(level + 1, levels - 1))],
            [like(message), like(message), dma((2,))],
        )
        if level < levels - 1:
            message = results[-1]
            static_got = swap(message, mask_of(level + 1), 1)
        if level > 1:
            near, far = to_core(results[0], 0), to_core(results[0], 0, 3)
        cut = width + inner

        width = (levels - 1 - level) * rank
        outs = [sds((half, 2 * rank if level == 1 else rank), BF)]
        if width:
            outs.append(sds((half, width), BF))
        results = call(
            lambda *refs, l=level: step_body(*refs, level=l),
            outs,
            [own, other, near, far],
            [VMEM, VMEM, VMEM, VMEM],
        )
        gathered.append(results[0])
        if width:
            own, static_got = lax.optimization_barrier((results[1], static_got))
            send = own
        if level == early:
            state = spread_out(state, gathered, 1, zero)
    return spread_out(state, gathered[early:], early + 1, None)


def solution(mesh):
    return jax.shard_map(
        on_device,
        mesh=mesh,
        in_specs=(
            P(AXIS, None),
            P(AXIS, None, None),
            P(None, AXIS, None),
            P(None, AXIS, None),
            P(None, AXIS, None),
        ),
        out_specs=P(AXIS, None),
        check_vma=False,
    )
```

```python
import jax
import jax.numpy as jnp
from jax import lax
from jax.experimental import pallas as pl
from jax.experimental.pallas import tpu as pltpu
from jax.sharding import PartitionSpec as P

BF = jnp.bfloat16
F32 = jnp.float32
AXIS = "seq"
MASKS = {3: 12, 6: 96, 8: 384}


def mask_of(level):
    return MASKS.get(level, 1 << level)


def swap(value, mask, core):
    pairs = [(d, d ^ mask) for d in range(lax.axis_size(AXIS)) if d & 1 == core]
    return lax.ppermute(value, AXIS, pairs)


def to_core(value, core, mask=1):
    pairs = [(d ^ mask, d) for d in range(lax.axis_size(AXIS)) if d & 1 == core]
    return lax.ppermute(value, AXIS, pairs)


def dot(a, b, dims):
    return lax.dot_general(a, b, (dims, ((), ())), preferred_element_type=F32)


NN = ((1,), (0,))
NT = ((1,), (1,))
TN = ((0,), (0,))


VMEM = pl.BlockSpec(memory_space=pltpu.VMEM)
ANY = pl.BlockSpec(memory_space=pl.ANY)


def call(body, outs, args, specs, scratch=(), grid=(1,), out_specs=None):
    return pl.pallas_call(
        body,
        out_shape=outs,
        grid=grid,
        in_specs=specs,
        out_specs=out_specs or [VMEM] * len(outs),
        scratch_shapes=list(scratch),
        compiler_params=pltpu.CompilerParams(vmem_limit_bytes=40 * 2**20),
        cost_estimate=pl.CostEstimate(
            flops=0, bytes_accessed=sum(a.size * a.dtype.itemsize for a in args), transcendentals=0
        ),
    )(*args)


def sds(shape, dtype):
    return jax.ShapeDtypeStruct(shape, dtype)


def like(array):
    return pltpu.VMEM(array.shape, array.dtype)


def bit(level):
    return lax.axis_index(AXIS) >> level & 1


def rows_of(part, count):
    return pl.ds(pl.multiple_of(part * count, count), count)


def blocks_body(project_ref, spread_ref, static_ref):
    levels = project_ref.shape[0]
    at = 0
    for low in range(1, levels - 1):
        spread = spread_ref[low]
        for high in range(low + 1, levels):
            block = dot(spread, project_ref[high], TN)
            static_ref[:, at : at + block.shape[1]] = block.astype(BF)
            at += block.shape[1]


def leaf_body(inverse_ref, right_ref, project_ref, state_ref, sums_ref):
    state = dot(inverse_ref[0], right_ref[...], NN)
    state_ref[...] = state
    sums_ref[...] = dot(project_ref[0], state.astype(BF), TN).astype(BF)


def first_body(state_ref, stacked_ref, capacity_ref, spread_ref, project_ref, first_ref, sums_ref):
    coefficients = dot(capacity_ref[0], stacked_ref[...], NN).astype(BF)
    first_ref[...] = coefficients
    rounded = (state_ref[...] - dot(spread_ref[0], coefficients, NN)).astype(BF)
    for level in range(1, project_ref.shape[0]):
        block = dot(rounded, project_ref[level], TN)
        rank = block.shape[1]
        sums_ref[:, (level - 1) * rank : level * rank] = block.astype(BF)


def fetch(pairs, sems):
    copies = [pltpu.make_async_copy(a, b, sems.at[i]) for i, (a, b) in enumerate(pairs)]
    for copy in copies:
        copy.start()
    for copy in copies:
        copy.wait()


def merge_body(own_any, other_any, keep_ref, send_ref, own, other, sems):
    @pl.when(bit(0) == 0)
    def _():
        fetch([(own_any, own), (other_any, other)], sems)
        side = bit(1)
        count = keep_ref.shape[0]
        for part, out_ref in ((side, keep_ref), (1 - side, send_ref)):
            rows = rows_of(part, count)
            out_ref[...] = (own[rows, :].astype(F32) + other[rows, :].astype(F32)).astype(BF)


def cut_body(own_any, other_any, capacity_ref, message_ref, keep_ref, own, other, sems, *, first, last):
    @pl.when(bit(0) == 1)
    def _():
        fetch([(own_any, own), (other_any, other)], sems)
        inner = capacity_ref.shape[2]
        count = own.shape[0] // 2
        part = (own.shape[1] - last) // 2

        def total(rows, low, high):
            return (own[rows, low:high].astype(F32) + other[rows, low:high].astype(F32)).astype(BF)

        message_ref[:, :first] = total(slice(None), 0, first)
        message_ref[:, first : first + inner] = capacity_ref[0]
        message_ref[:, first + inner : last + inner] = total(slice(None), first, last)
        for place, out_ref, at in ((bit(1), keep_ref, 0), (1 - bit(1), message_ref, last + inner)):
            rows = rows_of(place, count)
            out_ref[:count, at:] = total(rows, last, last + part)
            out_ref[count:, at:] = total(rows, last + part, last + 2 * part)


def static_body(own_any, other_any, keep_ref, capacity_ref, *refs, cut, width, outs, kept, plain):
    out_refs, (own, other, sems) = refs[:outs], refs[outs:]

    @pl.when(bit(0) == 1)
    def _():
        fetch([(own_any, own), (other_any, other)], sems)
        count = own.shape[0]
        inner = capacity_ref.shape[2]
        out_refs[0][:count, :] = own[:, :cut]
        out_refs[0][count:, :] = other[:, :cut]
        if outs == 1:
            return
        message_ref = out_refs[1]

        def total(low, high):
            return (own[:, low:high].astype(F32) + other[:, low:high].astype(F32)).astype(BF)

        if plain:
            message_ref[...] = total(cut, own.shape[1])
            return
        if width:
            message_ref[:, :width] = total(cut, cut + width)
        message_ref[:, width : width + inner] = capacity_ref[0]
        end = own.shape[1] - kept
        if end > cut + width:
            message_ref[:, width + inner : end - cut + inner] = total(cut + width, end)
        if kept:
            rest = keep_ref[...].astype(F32) + other[:, end:].astype(F32)
            message_ref[:, end - cut + inner :] = rest.astype(BF)


def join_body(own_ref, other_ref, capacity_ref, message_ref, *, width):
    @pl.when(bit(0) == 1)
    def _():
        inner = capacity_ref.shape[2]
        part = own_ref.shape[1]
        count = own_ref.shape[0] // 2
        message_ref[:, width : width + inner] = capacity_ref[0]
        for place, ref in ((bit(1), own_ref), (1 - bit(1), other_ref)):
            rows = rows_of(place, count)
            for half in range(2):
                low, high = half * part, (half + 1) * part
                middle = min(max(low, width), high)
                block = ref[half * count : (half + 1) * count, :]
                if middle > low:
                    message_ref[rows, low:middle] = block[:, : middle - low]
                if high > middle:
                    message_ref[rows, middle + inner : high + inner] = block[:, middle - low :]


def step_body(own_ref, other_ref, static_ref, *out_refs, level):
    rank = static_ref.shape[0] // 2
    width = own_ref.shape[1] - rank

    @pl.when(bit(0) == 0)
    def _():
        lower = bit(level) == 0
        own, other = own_ref[:, :rank], other_ref[:, :rank]
        stacked = jnp.concatenate([jnp.where(lower, own, other), jnp.where(lower, other, own)], 1)
        both = dot(stacked, static_ref[:, width:], NT).astype(BF)
        out_refs[0][...] = both[:, : out_refs[0].shape[1]]
        if width:
            total = own_ref[:, rank:].astype(F32) + other_ref[:, rank:].astype(F32)
            out_refs[1][...] = (total - dot(both, static_ref[:, :width], NN)).astype(BF)


def spread_body(state_ref, *refs, count, zero):
    spreads, (near0_ref, far0_ref, near1_ref, far1_ref), rest = refs[:count], refs[count : count + 4], refs[count + 4 :]
    out_ref = rest[-1]
    zero_core = bit(0) == 0
    first = bit(1) == 0
    total = state_ref[...]
    if zero:
        total = total - dot(rest[0][0], rest[1][...], NN)
    for at in range(0, count, 2):
        left, right = [], []
        for index in range(at, min(at + 2, count)):
            near = jnp.where(zero_core, near0_ref[index], near1_ref[index])
            far = jnp.where(zero_core, far0_ref[index], far1_ref[index])
            left.append(spreads[index][0])
            right.append(jnp.concatenate([jnp.where(first, near, far), jnp.where(first, far, near)], 0))
        total = total - dot(jnp.concatenate(left, 1), jnp.concatenate(right, 1), NT)
    out_ref[...] = total


def on_device(right_side, leaf_inverse, project_rows, spread_rows, capacity):
    levels, samples, rank = project_rows.shape
    columns = right_side.shape[1]
    inner = capacity.shape[2]
    size = lax.axis_size(AXIS)
    dma = pltpu.SemaphoreType.DMA

    def level_block(array, level):
        return pl.BlockSpec((1,) + array.shape[1:], lambda i: (level, 0, 0))

    pairs = (levels - 1) * (levels - 2) // 2
    (static,) = call(
        blocks_body, [sds((rank, pairs * rank), BF)], [project_rows, spread_rows], [VMEM, VMEM]
    )
    static_other = to_core(static, 1)
    state, sums = call(
        leaf_body,
        [sds((samples, columns), F32), sds((rank, columns), BF)],
        [leaf_inverse, right_side, project_rows],
        [VMEM, VMEM, level_block(project_rows, 0)],
    )
    static_other, sums = lax.optimization_barrier((static_other, sums))
    stacked = lax.all_gather(
        sums, AXIS, axis_index_groups=[[d, d + 1] for d in range(0, size, 2)], tiled=True
    )
    def blocks(low, high):
        return sum(levels - 1 - level for level in range(low, min(high, levels - 1))) * rank

    split = 4
    rest = blocks(split, levels) // 2
    message, keep = call(
        lambda *refs: cut_body(*refs, first=blocks(1, 2), last=blocks(1, split)),
        [sds((rank, blocks(1, split) + inner + rest), BF), sds((rank, rest), BF)],
        [static, static_other, capacity],
        [ANY, ANY, level_block(capacity, 1)],
        [like(static), like(static), dma((2,))],
    )
    stacked, message = lax.optimization_barrier((stacked, message))
    static_got = swap(message, mask_of(1), 1)
    zero, sums = call(
        first_body,
        [sds((rank, columns), BF), sds((columns, (levels - 1) * rank), BF)],
        [state, stacked, capacity, spread_rows, project_rows],
        [VMEM, VMEM, level_block(capacity, 0), level_block(spread_rows, 0), VMEM],
    )
    half = columns // 2
    own, send = call(
        merge_body,
        [sds((half, (levels - 1) * rank), BF)] * 2,
        [sums, to_core(sums, 0)],
        [ANY, ANY],
        [like(sums), like(sums), dma((2,))],
    )

    def spread_out(state, mine, base, zero):
        near0 = jnp.stack([c[:, :rank] for c in mine])
        theirs = jnp.stack([c[:, -rank:] for c in mine])
        far0 = swap(theirs, 2, 0)
        near1 = to_core(near0, 1)
        far1 = to_core(theirs, 1, 3)
        count = len(mine)
        tile = samples // 2

        def spread_block(level):
            return pl.BlockSpec((1, tile, rank), lambda i: (level, i, 0))

        whole = pl.BlockSpec((tile, columns), lambda i: (i, 0))
        args = [state] + [spread_rows] * count + [near0, far0, near1, far1]
        specs = [whole] + [spread_block(base + i) for i in range(count)] + [VMEM] * 4
        if zero is not None:
            args += [spread_rows, zero]
            specs += [spread_block(0), VMEM]
        return call(
            lambda *refs: spread_body(*refs, count=count, zero=zero is not None),
            [sds((samples, columns), F32)],
            args,
            specs,
            grid=(2,),
            out_specs=[whole],
        )[0]

    gathered = []
    early = levels - 3
    for level in range(1, levels):
        other = swap(send, mask_of(level), 0)
        plain = level == split - 1 and rest > 0
        outs = [sds((2 * rank, blocks(level, level + 1) + inner), BF)]
        if plain:
            outs.append(sds((rank, rest), BF))
        elif level < levels - 1:
            late = rest if level < split else blocks(level + 2, levels)
            outs.append(sds((rank, blocks(level + 1, max(split, level + 2) if level < split else level + 2) + inner + late), BF))
        results = call(
            lambda *refs, l=level, n=len(outs), p=plain: static_body(
                *refs, cut=blocks(l, l + 1) + inner, width=blocks(l + 1, l + 2), outs=n, kept=rest if l == 1 else 0, plain=p
            ),
            outs,
            [message, static_got, keep, capacity],
            [ANY, ANY, VMEM, level_block(capacity, min(level + 1, levels - 1))],
            [like(message), like(message), dma((2,))],
        )
        both = results[0]
        static_block = to_core(both, 0)
        if plain:
            (message,) = call(
                lambda *refs: join_body(*refs, width=blocks(split, split + 1)),
                [sds((rank, 2 * rest + inner), BF)],
                [results[1], swap(results[1], 2, 1), capacity],
                [VMEM, VMEM, level_block(capacity, split)],
            )
        elif level < levels - 1:
            message = results[1]
        if level < levels - 1:
            static_got = swap(message, mask_of(level + 1), 1)

        width = (levels - 1 - level) * rank
        outs = [sds((half, 2 * rank if level == 1 else rank), BF)]
        if width:
            outs.append(sds((half, width), BF))
        results = call(
            lambda *refs, l=level: step_body(*refs, level=l),
            outs,
            [own, other, static_block],
            [VMEM, VMEM, VMEM],
        )
        gathered.append(results[0])
        if width:
            own = results[1]
            send = own
        if level == early:
            state = spread_out(state, gathered, 1, zero)
    return spread_out(state, gathered[early:], early + 1, None)


def solution(mesh):
    return jax.shard_map(
        on_device,
        mesh=mesh,
        in_specs=(
            P(AXIS, None),
            P(AXIS, None, None),
            P(None, AXIS, None),
            P(None, AXIS, None),
            P(None, AXIS, None),
        ),
        out_specs=P(AXIS, None),
        check_vma=False,
    )
```

```python
import jax
import jax.numpy as jnp
from jax import lax
from jax.experimental import pallas as pl
from jax.experimental.pallas import tpu as pltpu
from jax.sharding import PartitionSpec as P

BF = jnp.bfloat16
F32 = jnp.float32
AXIS = "seq"
MASKS = {3: 12, 6: 96, 8: 384}


def mask_of(level):
    return MASKS.get(level, 1 << level)


def swap(value, mask, core):
    pairs = [(d, d ^ mask) for d in range(lax.axis_size(AXIS)) if d & 1 == core]
    return lax.ppermute(value, AXIS, pairs)


def to_core(value, core, mask=1):
    pairs = [(d ^ mask, d) for d in range(lax.axis_size(AXIS)) if d & 1 == core]
    return lax.ppermute(value, AXIS, pairs)


def dot(a, b, dims):
    return lax.dot_general(a, b, (dims, ((), ())), preferred_element_type=F32)


NN = ((1,), (0,))
NT = ((1,), (1,))
TN = ((0,), (0,))


VMEM = pl.BlockSpec(memory_space=pltpu.VMEM)
ANY = pl.BlockSpec(memory_space=pl.ANY)


def call(body, outs, args, specs, scratch=(), grid=(1,), out_specs=None):
    return pl.pallas_call(
        body,
        out_shape=outs,
        grid=grid,
        in_specs=specs,
        out_specs=out_specs or [VMEM] * len(outs),
        scratch_shapes=list(scratch),
        compiler_params=pltpu.CompilerParams(vmem_limit_bytes=40 * 2**20),
        cost_estimate=pl.CostEstimate(
            flops=0, bytes_accessed=sum(a.size * a.dtype.itemsize for a in args), transcendentals=0
        ),
    )(*args)


def sds(shape, dtype):
    return jax.ShapeDtypeStruct(shape, dtype)


def like(array):
    return pltpu.VMEM(array.shape, array.dtype)


def bit(level):
    return lax.axis_index(AXIS) >> level & 1


def rows_of(part, count):
    return pl.ds(pl.multiple_of(part * count, count), count)


def blocks_body(project_ref, spread_ref, static_ref):
    levels = project_ref.shape[0]
    at = 0
    for low in range(1, levels - 1):
        spread = spread_ref[low]
        for high in range(low + 1, levels):
            block = dot(spread, project_ref[high], TN)
            static_ref[:, at : at + block.shape[1]] = block.astype(BF)
            at += block.shape[1]


def leaf_body(inverse_ref, right_ref, project_ref, state_ref, sums_ref):
    state = dot(inverse_ref[0], right_ref[...], NN)
    state_ref[...] = state
    sums_ref[...] = dot(project_ref[0], state.astype(BF), TN).astype(BF)


def first_body(state_ref, stacked_ref, capacity_ref, spread_ref, project_ref, first_ref, sums_ref):
    coefficients = dot(capacity_ref[0], stacked_ref[...], NN).astype(BF)
    first_ref[...] = coefficients
    rounded = (state_ref[...] - dot(spread_ref[0], coefficients, NN)).astype(BF)
    for level in range(1, project_ref.shape[0]):
        block = dot(rounded, project_ref[level], TN)
        rank = block.shape[1]
        sums_ref[:, (level - 1) * rank : level * rank] = block.astype(BF)


def fetch(pairs, sems):
    copies = [pltpu.make_async_copy(a, b, sems.at[i]) for i, (a, b) in enumerate(pairs)]
    for copy in copies:
        copy.start()
    for copy in copies:
        copy.wait()


def merge_body(own_any, other_any, keep_ref, send_ref, own, other, sems):
    @pl.when(bit(0) == 0)
    def _():
        fetch([(own_any, own), (other_any, other)], sems)
        side = bit(1)
        count = keep_ref.shape[0]
        for part, out_ref in ((side, keep_ref), (1 - side, send_ref)):
            rows = rows_of(part, count)
            out_ref[...] = (own[rows, :].astype(F32) + other[rows, :].astype(F32)).astype(BF)


def cut_body(own_any, other_any, capacity_ref, message_ref, keep_ref, own, other, sems, *, first, last):
    @pl.when(bit(0) == 1)
    def _():
        fetch([(own_any, own), (other_any, other)], sems)
        inner = capacity_ref.shape[2]
        count = own.shape[0] // 2
        part = (own.shape[1] - last) // 2

        def total(rows, low, high):
            return (own[rows, low:high].astype(F32) + other[rows, low:high].astype(F32)).astype(BF)

        message_ref[:, :first] = total(slice(None), 0, first)
        message_ref[:, first : first + inner] = capacity_ref[0]
        message_ref[:, first + inner : last + inner] = total(slice(None), first, last)
        for place, out_ref, at in ((bit(1), keep_ref, 0), (1 - bit(1), message_ref, last + inner)):
            rows = rows_of(place, count)
            out_ref[:count, at:] = total(rows, last, last + part)
            out_ref[count:, at:] = total(rows, last + part, last + 2 * part)


def static_body(own_any, other_any, keep_ref, capacity_ref, *refs, cut, width, outs, kept):
    out_refs, (own, other, sems) = refs[:outs], refs[outs:]

    @pl.when(bit(0) == 1)
    def _():
        fetch([(own_any, own), (other_any, other)], sems)
        count = own.shape[0]
        inner = capacity_ref.shape[2]
        out_refs[0][:count, :] = own[:, :cut]
        out_refs[0][count:, :] = other[:, :cut]
        if outs == 1:
            return
        message_ref = out_refs[1]

        def total(low, high):
            return (own[:, low:high].astype(F32) + other[:, low:high].astype(F32)).astype(BF)

        if width:
            message_ref[:, :width] = total(cut, cut + width)
        message_ref[:, width : width + inner] = capacity_ref[0]
        end = own.shape[1] - kept
        if end > cut + width:
            message_ref[:, width + inner : end - cut + inner] = total(cut + width, end)
        if kept:
            rest = keep_ref[...].astype(F32) + other[:, end:].astype(F32)
            message_ref[:, end - cut + inner :] = rest.astype(BF)


def tail_body(own_any, other_any, out_ref, own, other, sems, *, cut):
    @pl.when(bit(0) == 1)
    def _():
        fetch([(own_any, own), (other_any, other)], sems)
        out_ref[...] = (own[:, cut:].astype(F32) + other[:, cut:].astype(F32)).astype(BF)


def join_body(own_ref, other_ref, capacity_ref, message_ref, *, width):
    @pl.when(bit(0) == 1)
    def _():
        inner = capacity_ref.shape[2]
        part = own_ref.shape[1]
        count = own_ref.shape[0] // 2
        message_ref[:, width : width + inner] = capacity_ref[0]
        for place, ref in ((bit(1), own_ref), (1 - bit(1), other_ref)):
            rows = rows_of(place, count)
            for half in range(2):
                low, high = half * part, (half + 1) * part
                middle = min(max(low, width), high)
                block = ref[half * count : (half + 1) * count, :]
                if middle > low:
                    message_ref[rows, low:middle] = block[:, : middle - low]
                if high > middle:
                    message_ref[rows, middle + inner : high + inner] = block[:, middle - low :]


def step_body(own_ref, other_ref, static_ref, *out_refs, level):
    rank = static_ref.shape[0] // 2
    width = own_ref.shape[1] - rank

    @pl.when(bit(0) == 0)
    def _():
        lower = bit(level) == 0
        own, other = own_ref[:, :rank], other_ref[:, :rank]
        stacked = jnp.concatenate([jnp.where(lower, own, other), jnp.where(lower, other, own)], 1)
        both = dot(stacked, static_ref[:, width:], NT).astype(BF)
        out_refs[0][...] = both[:, : out_refs[0].shape[1]]
        if width:
            total = own_ref[:, rank:].astype(F32) + other_ref[:, rank:].astype(F32)
            out_refs[1][...] = (total - dot(both, static_ref[:, :width], NN)).astype(BF)


def spread_body(state_ref, *refs, count, zero):
    spreads, (near0_ref, far0_ref, near1_ref, far1_ref), rest = refs[:count], refs[count : count + 4], refs[count + 4 :]
    out_ref = rest[-1]
    zero_core = bit(0) == 0
    first = bit(1) == 0
    total = state_ref[...]
    if zero:
        total = total - dot(rest[0][0], rest[1][...], NN)
    for at in range(0, count, 2):
        left, right = [], []
        for index in range(at, min(at + 2, count)):
            near = jnp.where(zero_core, near0_ref[index], near1_ref[index])
            far = jnp.where(zero_core, far0_ref[index], far1_ref[index])
            left.append(spreads[index][0])
            right.append(jnp.concatenate([jnp.where(first, near, far), jnp.where(first, far, near)], 0))
        total = total - dot(jnp.concatenate(left, 1), jnp.concatenate(right, 1), NT)
    out_ref[...] = total


def on_device(right_side, leaf_inverse, project_rows, spread_rows, capacity):
    levels, samples, rank = project_rows.shape
    columns = right_side.shape[1]
    inner = capacity.shape[2]
    size = lax.axis_size(AXIS)
    dma = pltpu.SemaphoreType.DMA

    def level_block(array, level):
        return pl.BlockSpec((1,) + array.shape[1:], lambda i: (level, 0, 0))

    pairs = (levels - 1) * (levels - 2) // 2
    (static,) = call(
        blocks_body, [sds((rank, pairs * rank), BF)], [project_rows, spread_rows], [VMEM, VMEM]
    )
    static_other = to_core(static, 1)
    state, sums = call(
        leaf_body,
        [sds((samples, columns), F32), sds((rank, columns), BF)],
        [leaf_inverse, right_side, project_rows],
        [VMEM, VMEM, level_block(project_rows, 0)],
    )
    static_other, sums = lax.optimization_barrier((static_other, sums))
    stacked = lax.all_gather(
        sums, AXIS, axis_index_groups=[[d, d + 1] for d in range(0, size, 2)], tiled=True
    )
    def blocks(low, high):
        return sum(levels - 1 - level for level in range(low, min(high, levels - 1))) * rank

    split = 4
    rest = blocks(split, levels) // 2
    message, keep = call(
        lambda *refs: cut_body(*refs, first=blocks(1, 2), last=blocks(1, split)),
        [sds((rank, blocks(1, split) + inner + rest), BF), sds((rank, rest), BF)],
        [static, static_other, capacity],
        [ANY, ANY, level_block(capacity, 1)],
        [like(static), like(static), dma((2,))],
    )
    stacked, message = lax.optimization_barrier((stacked, message))
    static_got = swap(message, mask_of(1), 1)
    zero, sums = call(
        first_body,
        [sds((rank, columns), BF), sds((columns, (levels - 1) * rank), BF)],
        [state, stacked, capacity, spread_rows, project_rows],
        [VMEM, VMEM, level_block(capacity, 0), level_block(spread_rows, 0), VMEM],
    )
    half = columns // 2
    own, send = call(
        merge_body,
        [sds((half, (levels - 1) * rank), BF)] * 2,
        [sums, to_core(sums, 0)],
        [ANY, ANY],
        [like(sums), like(sums), dma((2,))],
    )

    def stacks(mine):
        return jnp.stack([c[:, :rank] for c in mine]), jnp.stack([c[:, -rank:] for c in mine])

    def spread_out(state, near0, theirs, far0, base, zero):
        near1 = to_core(near0, 1)
        far1 = to_core(theirs, 1, 3)
        count = near0.shape[0]
        tile = samples // 2

        def spread_block(level):
            return pl.BlockSpec((1, tile, rank), lambda i: (level, i, 0))

        whole = pl.BlockSpec((tile, columns), lambda i: (i, 0))
        args = [state] + [spread_rows] * count + [near0, far0, near1, far1]
        specs = [whole] + [spread_block(base + i) for i in range(count)] + [VMEM] * 4
        if zero is not None:
            args += [spread_rows, zero]
            specs += [spread_block(0), VMEM]
        return call(
            lambda *refs: spread_body(*refs, count=count, zero=zero is not None),
            [sds((samples, columns), F32)],
            args,
            specs,
            grid=(2,),
            out_specs=[whole],
        )[0]

    gathered = []
    early = levels - 3
    for level in range(1, levels):
        if level == split - 1:
            other = swap(send, mask_of(level), 0)
        plain = level == split - 1 and rest > 0
        outs = [sds((2 * rank, blocks(level, level + 1) + inner), BF)]
        if level < levels - 1 and not plain:
            late = rest if level < split else blocks(level + 2, levels)
            outs.append(sds((rank, blocks(level + 1, max(split, level + 2) if level < split else level + 2) + inner + late), BF))
        results = call(
            lambda *refs, l=level, n=len(outs): static_body(
                *refs, cut=blocks(l, l + 1) + inner, width=blocks(l + 1, l + 2), outs=n, kept=rest if l == 1 else 0
            ),
            outs,
            [message, static_got, keep, capacity],
            [ANY, ANY, VMEM, level_block(capacity, min(level + 1, levels - 1))],
            [like(message), like(message), dma((2,))],
        )
        static_block = to_core(results[0], 0)
        if plain:
            static_got, other, static_block = lax.optimization_barrier((static_got, other, static_block))
            (tail,) = call(
                lambda *refs, c=blocks(level, level + 1) + inner: tail_body(*refs, cut=c),
                [sds((rank, rest), BF)],
                [message, static_got],
                [ANY, ANY],
                [like(message), like(message), dma((2,))],
            )
            (message,) = call(
                lambda *refs: join_body(*refs, width=blocks(split, split + 1)),
                [sds((rank, 2 * rest + inner), BF)],
                [tail, swap(tail, 2, 1), capacity],
                [VMEM, VMEM, level_block(capacity, split)],
            )
        elif level < levels - 1:
            message = results[1]
        if level < levels - 1:
            static_got = swap(message, mask_of(level + 1), 1)

        if level != split - 1:
            other = swap(send, mask_of(level), 0)
        width = (levels - 1 - level) * rank
        outs = [sds((half, 2 * rank if level == 1 else rank), BF)]
        if width:
            outs.append(sds((half, width), BF))
        results = call(
            lambda *refs, l=level: step_body(*refs, level=l),
            outs,
            [own, other, static_block],
            [VMEM, VMEM, VMEM],
        )
        gathered.append(results[0])
        if width:
            own = results[1]
            if level < split - 1:
                own, static_got = lax.optimization_barrier((own, static_got))
            send = own
        if level == early:
            near0, theirs = stacks(gathered)
            far0 = swap(theirs, 2, 0)
        if level == early + 1:
            near0, theirs, _ = lax.optimization_barrier((near0, theirs, gathered[-1]))
            state = spread_out(state, near0, theirs, far0, 1, zero)
    near0, theirs = stacks(gathered[early:])
    return spread_out(state, near0, theirs, swap(theirs, 2, 0), early + 1, None)


def solution(mesh):
    return jax.shard_map(
        on_device,
        mesh=mesh,
        in_specs=(
            P(AXIS, None),
            P(AXIS, None, None),
            P(None, AXIS, None),
            P(None, AXIS, None),
            P(None, AXIS, None),
        ),
        out_specs=P(AXIS, None),
        check_vma=False,
    )
```

```python
import jax
import jax.numpy as jnp
from jax import lax
from jax.experimental import pallas as pl
from jax.experimental.pallas import tpu as pltpu
from jax.sharding import PartitionSpec as P

BF = jnp.bfloat16
F32 = jnp.float32
AXIS = "seq"
MASKS = {3: 12, 6: 96, 8: 384}


def mask_of(level):
    return MASKS.get(level, 1 << level)


def swap(value, mask, core):
    pairs = [(d, d ^ mask) for d in range(lax.axis_size(AXIS)) if d & 1 == core]
    return lax.ppermute(value, AXIS, pairs)


def to_core(value, core, mask=1):
    pairs = [(d ^ mask, d) for d in range(lax.axis_size(AXIS)) if d & 1 == core]
    return lax.ppermute(value, AXIS, pairs)


def dot(a, b, dims):
    return lax.dot_general(a, b, (dims, ((), ())), preferred_element_type=F32)


NN = ((1,), (0,))
NT = ((1,), (1,))
TN = ((0,), (0,))


VMEM = pl.BlockSpec(memory_space=pltpu.VMEM)
ANY = pl.BlockSpec(memory_space=pl.ANY)


def call(body, outs, args, specs, scratch=(), grid=(1,), out_specs=None):
    return pl.pallas_call(
        body,
        out_shape=outs,
        grid=grid,
        in_specs=specs,
        out_specs=out_specs or [VMEM] * len(outs),
        scratch_shapes=list(scratch),
        compiler_params=pltpu.CompilerParams(vmem_limit_bytes=40 * 2**20),
        cost_estimate=pl.CostEstimate(
            flops=0, bytes_accessed=sum(a.size * a.dtype.itemsize for a in args), transcendentals=0
        ),
    )(*args)


def sds(shape, dtype):
    return jax.ShapeDtypeStruct(shape, dtype)


def like(array):
    return pltpu.VMEM(array.shape, array.dtype)


def bit(level):
    return lax.axis_index(AXIS) >> level & 1


def rows_of(part, count):
    return pl.ds(pl.multiple_of(part * count, count), count)


def blocks_body(project_ref, spread_ref, static_ref):
    levels = project_ref.shape[0]
    at = 0
    for low in range(1, levels - 1):
        spread = spread_ref[low]
        for high in range(low + 1, levels):
            block = dot(spread, project_ref[high], TN)
            static_ref[:, at : at + block.shape[1]] = block.astype(BF)
            at += block.shape[1]


def leaf_body(inverse_ref, right_ref, project_ref, state_ref, sums_ref):
    state = dot(inverse_ref[0], right_ref[...], NN)
    state_ref[...] = state
    sums_ref[...] = dot(project_ref[0], state.astype(BF), TN).astype(BF)


def first_body(state_ref, stacked_ref, capacity_ref, spread_ref, project_ref, first_ref, sums_ref):
    coefficients = dot(capacity_ref[0], stacked_ref[...], NN).astype(BF)
    first_ref[...] = coefficients
    rounded = (state_ref[...] - dot(spread_ref[0], coefficients, NN)).astype(BF)
    for level in range(1, project_ref.shape[0]):
        block = dot(rounded, project_ref[level], TN)
        rank = block.shape[1]
        sums_ref[:, (level - 1) * rank : level * rank] = block.astype(BF)


def fetch(pairs, sems):
    copies = [pltpu.make_async_copy(a, b, sems.at[i]) for i, (a, b) in enumerate(pairs)]
    for copy in copies:
        copy.start()
    for copy in copies:
        copy.wait()


def merge_body(own_any, other_any, keep_ref, send_ref, own, other, sems):
    @pl.when(bit(0) == 0)
    def _():
        fetch([(own_any, own), (other_any, other)], sems)
        side = bit(1)
        count = keep_ref.shape[0]
        for part, out_ref in ((side, keep_ref), (1 - side, send_ref)):
            rows = rows_of(part, count)
            out_ref[...] = (own[rows, :].astype(F32) + other[rows, :].astype(F32)).astype(BF)


def cut_body(own_any, other_any, capacity_ref, message_ref, own, other, sems, *, first):
    @pl.when(bit(0) == 1)
    def _():
        fetch([(own_any, own), (other_any, other)], sems)
        inner = capacity_ref.shape[2]
        for low, high, at in ((0, first, 0), (first, own.shape[1], first + inner)):
            total = own[:, low:high].astype(F32) + other[:, low:high].astype(F32)
            message_ref[:, at : at + high - low] = total.astype(BF)
        message_ref[:, first : first + inner] = capacity_ref[0]


def static_body(own_any, other_any, capacity_ref, *refs, cut, width, outs):
    out_refs, (own, other, sems) = refs[:outs], refs[outs:]

    @pl.when(bit(0) == 1)
    def _():
        fetch([(own_any, own), (other_any, other)], sems)
        count = own.shape[0]
        inner = capacity_ref.shape[2]
        out_refs[0][:count, :] = own[:, :cut]
        out_refs[0][count:, :] = other[:, :cut]
        if outs == 1:
            return
        message_ref = out_refs[1]

        def total(low, high):
            return (own[:, low:high].astype(F32) + other[:, low:high].astype(F32)).astype(BF)

        if width:
            message_ref[:, :width] = total(cut, cut + width)
        message_ref[:, width : width + inner] = capacity_ref[0]
        if own.shape[1] > cut + width:
            message_ref[:, width + inner :] = total(cut + width, own.shape[1])


def step_body(own_ref, other_ref, static_ref, *out_refs, level):
    rank = static_ref.shape[0] // 2
    width = own_ref.shape[1] - rank

    @pl.when(bit(0) == 0)
    def _():
        lower = bit(level) == 0
        own, other = own_ref[:, :rank], other_ref[:, :rank]
        stacked = jnp.concatenate([jnp.where(lower, own, other), jnp.where(lower, other, own)], 1)
        both = dot(stacked, static_ref[:, width:], NT).astype(BF)
        out_refs[0][...] = both[:, : out_refs[0].shape[1]]
        if width:
            total = own_ref[:, rank:].astype(F32) + other_ref[:, rank:].astype(F32)
            out_refs[1][...] = (total - dot(both, static_ref[:, :width], NN)).astype(BF)


def spread_body(state_ref, *refs, count, zero):
    spreads, (near0_ref, far0_ref, near1_ref, far1_ref), rest = refs[:count], refs[count : count + 4], refs[count + 4 :]
    out_ref = rest[-1]
    zero_core = bit(0) == 0
    first = bit(1) == 0
    total = state_ref[...]
    if zero:
        total = total - dot(rest[0][0], rest[1][...], NN)
    for at in range(0, count, 2):
        left, right = [], []
        for index in range(at, min(at + 2, count)):
            near = jnp.where(zero_core, near0_ref[index], near1_ref[index])
            far = jnp.where(zero_core, far0_ref[index], far1_ref[index])
            left.append(spreads[index][0])
            right.append(jnp.concatenate([jnp.where(first, near, far), jnp.where(first, far, near)], 0))
        total = total - dot(jnp.concatenate(left, 1), jnp.concatenate(right, 1), NT)
    out_ref[...] = total


def on_device(right_side, leaf_inverse, project_rows, spread_rows, capacity):
    levels, samples, rank = project_rows.shape
    columns = right_side.shape[1]
    inner = capacity.shape[2]
    size = lax.axis_size(AXIS)
    dma = pltpu.SemaphoreType.DMA

    def level_block(array, level):
        return pl.BlockSpec((1,) + array.shape[1:], lambda i: (level, 0, 0))

    pairs = (levels - 1) * (levels - 2) // 2
    (static,) = call(
        blocks_body, [sds((rank, pairs * rank), BF)], [project_rows, spread_rows], [VMEM, VMEM]
    )
    static_other = to_core(static, 1)
    state, sums = call(
        leaf_body,
        [sds((samples, columns), F32), sds((rank, columns), BF)],
        [leaf_inverse, right_side, project_rows],
        [VMEM, VMEM, level_block(project_rows, 0)],
    )
    static_other, sums = lax.optimization_barrier((static_other, sums))
    def blocks(low, high):
        return sum(levels - 1 - level for level in range(low, min(high, levels - 1))) * rank

    (message,) = call(
        lambda *refs: cut_body(*refs, first=blocks(1, 2)),
        [sds((rank, pairs * rank + inner), BF)],
        [static, static_other, capacity],
        [ANY, ANY, level_block(capacity, 1)],
        [like(static), like(static), dma((2,))],
    )
    static_got = swap(message, mask_of(1), 1)
    sums, message = lax.optimization_barrier((sums, message))
    stacked = lax.all_gather(
        sums, AXIS, axis_index_groups=[[d, d + 1] for d in range(0, size, 2)], tiled=True
    )
    zero, sums = call(
        first_body,
        [sds((rank, columns), BF), sds((columns, (levels - 1) * rank), BF)],
        [state, stacked, capacity, spread_rows, project_rows],
        [VMEM, VMEM, level_block(capacity, 0), level_block(spread_rows, 0), VMEM],
    )
    half = columns // 2
    own, send = call(
        merge_body,
        [sds((half, (levels - 1) * rank), BF)] * 2,
        [sums, to_core(sums, 0)],
        [ANY, ANY],
        [like(sums), like(sums), dma((2,))],
    )

    def stacks(mine):
        return jnp.stack([c[:, :rank] for c in mine]), jnp.stack([c[:, -rank:] for c in mine])

    def spread_out(state, near0, theirs, far0, base, zero):
        near1 = to_core(near0, 1)
        far1 = to_core(theirs, 1, 3)
        count = near0.shape[0]
        tile = samples // 2

        def spread_block(level):
            return pl.BlockSpec((1, tile, rank), lambda i: (level, i, 0))

        whole = pl.BlockSpec((tile, columns), lambda i: (i, 0))
        args = [state] + [spread_rows] * count + [near0, far0, near1, far1]
        specs = [whole] + [spread_block(base + i) for i in range(count)] + [VMEM] * 4
        if zero is not None:
            args += [spread_rows, zero]
            specs += [spread_block(0), VMEM]
        return call(
            lambda *refs: spread_body(*refs, count=count, zero=zero is not None),
            [sds((samples, columns), F32)],
            args,
            specs,
            grid=(2,),
            out_specs=[whole],
        )[0]

    gathered = []
    early = levels - 3
    for level in range(1, levels):
        outs = [sds((2 * rank, blocks(level, level + 1) + inner), BF)]
        if level < levels - 1:
            outs.append(sds((rank, blocks(level + 1, levels) + inner), BF))
        results = call(
            lambda *refs, l=level, n=len(outs): static_body(
                *refs, cut=blocks(l, l + 1) + inner, width=blocks(l + 1, l + 2), outs=n
            ),
            outs,
            [message, static_got, capacity],
            [ANY, ANY, level_block(capacity, min(level + 1, levels - 1))],
            [like(message), like(message), dma((2,))],
        )
        static_block = to_core(results[0], 0)
        if level < levels - 1:
            message = results[1]
            static_got = swap(message, mask_of(level + 1), 1)

        other = swap(send, mask_of(level), 0)
        width = (levels - 1 - level) * rank
        outs = [sds((half, 2 * rank if level == 1 else rank), BF)]
        if width:
            outs.append(sds((half, width), BF))
        results = call(
            lambda *refs, l=level: step_body(*refs, level=l),
            outs,
            [own, other, static_block],
            [VMEM, VMEM, VMEM],
        )
        gathered.append(results[0])
        if width:
            own = results[1]
            if level < 3:
                own, static_got = lax.optimization_barrier((own, static_got))
            send = own
        if level == early:
            near0, theirs = stacks(gathered)
            far0 = swap(theirs, 2, 0)
        if level == early + 1:
            near0, theirs, _ = lax.optimization_barrier((near0, theirs, gathered[-1]))
            state = spread_out(state, near0, theirs, far0, 1, zero)
    near0, theirs = stacks(gathered[early:])
    return spread_out(state, near0, theirs, swap(theirs, 2, 0), early + 1, None)


def solution(mesh):
    return jax.shard_map(
        on_device,
        mesh=mesh,
        in_specs=(
            P(AXIS, None),
            P(AXIS, None, None),
            P(None, AXIS, None),
            P(None, AXIS, None),
            P(None, AXIS, None),
        ),
        out_specs=P(AXIS, None),
        check_vma=False,
    )
```

```python
import jax
import jax.numpy as jnp
from jax import lax
from jax.experimental import pallas as pl
from jax.experimental.pallas import tpu as pltpu
from jax.sharding import PartitionSpec as P

BF = jnp.bfloat16
F32 = jnp.float32
AXIS = "seq"
MASKS = {3: 12, 6: 96, 8: 384}


def mask_of(level):
    return MASKS.get(level, 1 << level)


def swap(value, mask, core):
    pairs = [(d, d ^ mask) for d in range(lax.axis_size(AXIS)) if d & 1 == core]
    return lax.ppermute(value, AXIS, pairs)


def to_core(value, core, mask=1):
    pairs = [(d ^ mask, d) for d in range(lax.axis_size(AXIS)) if d & 1 == core]
    return lax.ppermute(value, AXIS, pairs)


def dot(a, b, dims):
    return lax.dot_general(a, b, (dims, ((), ())), preferred_element_type=F32)


NN = ((1,), (0,))
NT = ((1,), (1,))
TN = ((0,), (0,))


VMEM = pl.BlockSpec(memory_space=pltpu.VMEM)
ANY = pl.BlockSpec(memory_space=pl.ANY)


def call(body, outs, args, specs, scratch=(), grid=(1,), out_specs=None):
    return pl.pallas_call(
        body,
        out_shape=outs,
        grid=grid,
        in_specs=specs,
        out_specs=out_specs or [VMEM] * len(outs),
        scratch_shapes=list(scratch),
        compiler_params=pltpu.CompilerParams(vmem_limit_bytes=40 * 2**20),
        cost_estimate=pl.CostEstimate(
            flops=0, bytes_accessed=sum(a.size * a.dtype.itemsize for a in args), transcendentals=0
        ),
    )(*args)


def sds(shape, dtype):
    return jax.ShapeDtypeStruct(shape, dtype)


def like(array):
    return pltpu.VMEM(array.shape, array.dtype)


def bit(level):
    return lax.axis_index(AXIS) >> level & 1


def rows_of(part, count):
    return pl.ds(pl.multiple_of(part * count, count), count)


def blocks_body(project_ref, spread_ref, static_ref):
    levels = project_ref.shape[0]
    at = 0
    for low in range(1, levels - 1):
        spread = spread_ref[low]
        for high in range(low + 1, levels):
            block = dot(spread, project_ref[high], TN)
            static_ref[:, at : at + block.shape[1]] = block.astype(BF)
            at += block.shape[1]


def leaf_body(inverse_ref, right_ref, project_ref, state_ref, sums_ref):
    state = dot(inverse_ref[0], right_ref[...], NN)
    state_ref[...] = state
    sums_ref[...] = dot(project_ref[0], state.astype(BF), TN).astype(BF)


def first_body(state_ref, stacked_ref, capacity_ref, spread_ref, project_ref, first_ref, sums_ref):
    coefficients = dot(capacity_ref[0], stacked_ref[...], NN).astype(BF)
    first_ref[...] = coefficients
    rounded = (state_ref[...] - dot(spread_ref[0], coefficients, NN)).astype(BF)
    for level in range(1, project_ref.shape[0]):
        block = dot(rounded, project_ref[level], TN)
        rank = block.shape[1]
        sums_ref[:, (level - 1) * rank : level * rank] = block.astype(BF)


def fetch(pairs, sems):
    copies = [pltpu.make_async_copy(a, b, sems.at[i]) for i, (a, b) in enumerate(pairs)]
    for copy in copies:
        copy.start()
    for copy in copies:
        copy.wait()


def merge_body(own_any, other_any, keep_ref, send_ref, own, other, sems):
    @pl.when(bit(0) == 0)
    def _():
        fetch([(own_any, own), (other_any, other)], sems)
        side = bit(1)
        count = keep_ref.shape[0]
        for part, out_ref in ((side, keep_ref), (1 - side, send_ref)):
            rows = rows_of(part, count)
            out_ref[...] = (own[rows, :].astype(F32) + other[rows, :].astype(F32)).astype(BF)


def cut_body(own_any, other_any, capacity_ref, message_ref, own, other, sems, *, first):
    @pl.when(bit(0) == 1)
    def _():
        fetch([(own_any, own), (other_any, other)], sems)
        inner = capacity_ref.shape[2]
        for low, high, at in ((0, first, 0), (first, own.shape[1], first + inner)):
            total = own[:, low:high].astype(F32) + other[:, low:high].astype(F32)
            message_ref[:, at : at + high - low] = total.astype(BF)
        message_ref[:, first : first + inner] = capacity_ref[0]


def static_body(own_any, other_any, capacity_ref, *refs, cut, width, outs):
    out_refs, (own, other, sems) = refs[:outs], refs[outs:]

    @pl.when(bit(0) == 1)
    def _():
        fetch([(own_any, own), (other_any, other)], sems)
        count = own.shape[0]
        inner = capacity_ref.shape[2]
        out_refs[0][:count, :] = own[:, :cut]
        out_refs[0][count:, :] = other[:, :cut]
        if outs == 1:
            return
        message_ref = out_refs[1]

        def total(low, high):
            return (own[:, low:high].astype(F32) + other[:, low:high].astype(F32)).astype(BF)

        if width:
            message_ref[:, :width] = total(cut, cut + width)
        message_ref[:, width : width + inner] = capacity_ref[0]
        if own.shape[1] > cut + width:
            message_ref[:, width + inner :] = total(cut + width, own.shape[1])


def step_body(own_ref, other_ref, static_ref, *out_refs, level):
    rank = static_ref.shape[0] // 2
    width = own_ref.shape[1] - rank

    @pl.when(bit(0) == 0)
    def _():
        lower = bit(level) == 0
        own, other = own_ref[:, :rank], other_ref[:, :rank]
        stacked = jnp.concatenate([jnp.where(lower, own, other), jnp.where(lower, other, own)], 1)
        both = dot(stacked, static_ref[:, width:], NT).astype(BF)
        out_refs[0][...] = both[:, : out_refs[0].shape[1]]
        if width:
            total = own_ref[:, rank:].astype(F32) + other_ref[:, rank:].astype(F32)
            out_refs[1][...] = (total - dot(both, static_ref[:, :width], NN)).astype(BF)


def spread_body(state_ref, *refs, count, zero):
    spreads, (near0_ref, far0_ref, near1_ref, far1_ref), rest = refs[:count], refs[count : count + 4], refs[count + 4 :]
    out_ref = rest[-1]
    zero_core = bit(0) == 0
    first = bit(1) == 0
    total = state_ref[...]
    if zero:
        total = total - dot(rest[0][0], rest[1][...], NN)
    for at in range(0, count, 2):
        left, right = [], []
        for index in range(at, min(at + 2, count)):
            near = jnp.where(zero_core, near0_ref[index], near1_ref[index])
            far = jnp.where(zero_core, far0_ref[index], far1_ref[index])
            left.append(spreads[index][0])
            right.append(jnp.concatenate([jnp.where(first, near, far), jnp.where(first, far, near)], 0))
        total = total - dot(jnp.concatenate(left, 1), jnp.concatenate(right, 1), NT)
    out_ref[...] = total


def on_device(right_side, leaf_inverse, project_rows, spread_rows, capacity):
    levels, samples, rank = project_rows.shape
    columns = right_side.shape[1]
    inner = capacity.shape[2]
    size = lax.axis_size(AXIS)
    dma = pltpu.SemaphoreType.DMA

    def level_block(array, level):
        return pl.BlockSpec((1,) + array.shape[1:], lambda i: (level, 0, 0))

    pairs = (levels - 1) * (levels - 2) // 2
    (static,) = call(
        blocks_body, [sds((rank, pairs * rank), BF)], [project_rows, spread_rows], [VMEM, VMEM]
    )
    static_other = to_core(static, 1)
    state, sums = call(
        leaf_body,
        [sds((samples, columns), F32), sds((rank, columns), BF)],
        [leaf_inverse, right_side, project_rows],
        [VMEM, VMEM, level_block(project_rows, 0)],
    )
    static_other, sums = lax.optimization_barrier((static_other, sums))
    def blocks(low, high):
        return sum(levels - 1 - level for level in range(low, min(high, levels - 1))) * rank

    (message,) = call(
        lambda *refs: cut_body(*refs, first=blocks(1, 2)),
        [sds((rank, pairs * rank + inner), BF)],
        [static, static_other, capacity],
        [ANY, ANY, level_block(capacity, 1)],
        [like(static), like(static), dma((2,))],
    )
    static_got = swap(message, mask_of(1), 1)
    sums, message = lax.optimization_barrier((sums, message))
    stacked = lax.all_gather(
        sums, AXIS, axis_index_groups=[[d, d + 1] for d in range(0, size, 2)], tiled=True
    )
    zero, sums = call(
        first_body,
        [sds((rank, columns), BF), sds((columns, (levels - 1) * rank), BF)],
        [state, stacked, capacity, spread_rows, project_rows],
        [VMEM, VMEM, level_block(capacity, 0), level_block(spread_rows, 0), VMEM],
    )
    half = columns // 2
    own, send = call(
        merge_body,
        [sds((half, (levels - 1) * rank), BF)] * 2,
        [sums, to_core(sums, 0)],
        [ANY, ANY],
        [like(sums), like(sums), dma((2,))],
    )

    def stacks(mine):
        return jnp.stack([c[:, :rank] for c in mine]), jnp.stack([c[:, -rank:] for c in mine])

    def spread_out(state, near0, theirs, far0, base, zero):
        near1 = to_core(near0, 1)
        far1 = to_core(theirs, 1, 3)
        count = near0.shape[0]
        tile = samples // 2

        def spread_block(level):
            return pl.BlockSpec((1, tile, rank), lambda i: (level, i, 0))

        whole = pl.BlockSpec((tile, columns), lambda i: (i, 0))
        args = [state] + [spread_rows] * count + [near0, far0, near1, far1]
        specs = [whole] + [spread_block(base + i) for i in range(count)] + [VMEM] * 4
        if zero is not None:
            args += [spread_rows, zero]
            specs += [spread_block(0), VMEM]
        return call(
            lambda *refs: spread_body(*refs, count=count, zero=zero is not None),
            [sds((samples, columns), F32)],
            args,
            specs,
            grid=(2,),
            out_specs=[whole],
        )[0]

    gathered = []
    early = levels - 3
    for level in range(1, levels):
        outs = [sds((2 * rank, blocks(level, level + 1) + inner), BF)]
        if level < levels - 1:
            outs.append(sds((rank, blocks(level + 1, levels) + inner), BF))
        results = call(
            lambda *refs, l=level, n=len(outs): static_body(
                *refs, cut=blocks(l, l + 1) + inner, width=blocks(l + 1, l + 2), outs=n
            ),
            outs,
            [message, static_got, capacity],
            [ANY, ANY, level_block(capacity, min(level + 1, levels - 1))],
            [like(message), like(message), dma((2,))],
        )
        static_block = to_core(results[0], 0)
        if level < levels - 1:
            message = results[1]
            static_got = swap(message, mask_of(level + 1), 1)

        other = swap(send, mask_of(level), 0)
        width = (levels - 1 - level) * rank
        outs = [sds((half, 2 * rank if level == 1 else rank), BF)]
        if width:
            outs.append(sds((half, width), BF))
        results = call(
            lambda *refs, l=level: step_body(*refs, level=l),
            outs,
            [own, other, static_block],
            [VMEM, VMEM, VMEM],
        )
        gathered.append(results[0])
        if width:
            own = results[1]
            if level < 3:
                own, static_got = lax.optimization_barrier((own, static_got))
            send = own
        if level == early:
            near0, theirs = stacks(gathered)
            far0 = swap(theirs, 2, 0)
        if level == levels - 1:
            near0, theirs, last = lax.optimization_barrier((near0, theirs, gathered[-1]))
            gathered[-1] = last
            near_last, theirs_last = stacks(gathered[early:])
            far_last = swap(theirs_last, 2, 0)
            state = spread_out(state, near0, theirs, far0, 1, zero)
    return spread_out(state, near_last, theirs_last, far_last, early + 1, None)


def solution(mesh):
    return jax.shard_map(
        on_device,
        mesh=mesh,
        in_specs=(
            P(AXIS, None),
            P(AXIS, None, None),
            P(None, AXIS, None),
            P(None, AXIS, None),
            P(None, AXIS, None),
        ),
        out_specs=P(AXIS, None),
        check_vma=False,
    )
```
